128 devices in a mesh: dp: 8 (over y, core), seq: 16 (over x, z).
Axes of the slice: x: 4, y: 4, z: 4, core: 2. Of those that a mesh axis runs over, the one named last changes fastest.
Arguments:
- query: bfloat16 [8, 2048, 1536], P('dp', 'seq'), may hold values from -6 to 6
- key_in: bfloat16 [8, 2048, 1536], P('dp', 'seq'), may hold values from -6 to 6
- value: bfloat16 [8, 2048, 1536], P('dp', 'seq'), may hold values from -6 to 6
- grad_out: bfloat16 [8, 2048, 1536], P('dp', 'seq'), may hold values from -6 to 6
- expert_ids: int32 [8, 2048, 2], P('dp', 'seq'), may hold values from 0 to 15, all different within a row; in each aligned block of 128 rows (0 to 127, 128 to 255, ..., all dimensions but the last counted through in order) at most 18 rows name the same one
- gate_weights: float32 [8, 2048, 2], P('dp', 'seq'), may hold values from 0.25 to 1
- w_gate: bfloat16 [16, 1536, 4096], P('seq', None, 'dp'), may hold values from -0.15625 to 0.15625
- w_up: bfloat16 [16, 1536, 4096], P('seq', None, 'dp'), may hold values from -0.15625 to 0.15625
- w_down: bfloat16 [16, 4096, 1536], P('seq', 'dp'), may hold values from -0.09375 to 0.09375
Outputs:
- grad_query: bfloat16 [8, 2048, 1536], P('dp', 'seq')
- grad_key: bfloat16 [8, 2048, 1536], P('dp', 'seq')
- grad_value: bfloat16 [8, 2048, 1536], P('dp', 'seq')
- grad_down: bfloat16 [16, 4096, 1536], P('seq', 'dp')
The draws below stay inside these ranges and needn't reach their ends.
Inputs may be any that keep to these rules, and one draw needn't show every extreme that they name: `expert_ids`: each token names two different experts; among the 128 tokens of one device no expert is named more than 18 times, and in every draw some expert is named exactly 18 times by some device.
All inputs are finite; a program needn't handle non-finite values.
Results may differ from the reference program's by a relative error of at most 0.024.
Values may be sent and summed in bfloat16 or wider, within the bound.
A program may use at most 192 MiB of HBM per device.

```python
import math
import jax
import jax.numpy as jnp
import numpy as np
from jax import lax

HEADS = 16
HD = 96
D = 1536
FF = 4096
EXPERTS = 16
TOK = 128
C = 18
SEQ = 2048
CLIPS = 8
N_DP = 8
N_SEQ = 16


def aligned_rows(key):
    sign_key, place_key = jax.random.split(key)
    sign_pattern = jnp.where(jax.random.bernoulli(sign_key, 0.5, (CLIPS, 3, D)), 1.0, -1.0).astype(jnp.float32)
    positions = jax.vmap(lambda subkey: jax.random.permutation(subkey, SEQ))(jax.random.split(place_key, CLIPS))
    return (sign_pattern, positions.astype(jnp.int32))


def draw_query(key, part):
    sign_pattern, positions = aligned_rows(key)
    key = jax.random.fold_in(key, 3)
    background = jnp.clip(jax.random.normal(key, (CLIPS, SEQ, D), jnp.float32), -6.0, 6.0)
    clip_index = jnp.arange(CLIPS, dtype=jnp.int32)[:, None]
    result = background.at[clip_index, positions[:, 0:3]].set(6.0 * sign_pattern)
    return result.astype(jnp.bfloat16)


def draw_key_in(key, part):
    sign_pattern, positions = aligned_rows(key)
    key = jax.random.fold_in(key, 5)
    background = jnp.clip(jax.random.normal(key, (CLIPS, SEQ, D), jnp.float32), -6.0, 6.0)
    strength = jnp.array([2.5, 2.0, 1.75], jnp.float32)
    clip_index = jnp.arange(CLIPS, dtype=jnp.int32)[:, None]
    top_rows = strength[None, :, None] * sign_pattern
    near_rows = (strength[None, :, None] - 0.03125) * sign_pattern
    result = background.at[clip_index, positions[:, 3:6]].set(top_rows)
    result = result.at[clip_index, positions[:, 6:9]].set(near_rows)
    return result.astype(jnp.bfloat16)


def block_scale(key, extent, shards, smallest, high):
    gain = 1.0
    for axis_at, parts in shards:
        steps = jax.random.uniform(jax.random.fold_in(jax.random.fold_in(key, 6), axis_at), (parts,), jnp.float32, smallest / len(shards), high / len(shards))
        gain = gain * jnp.repeat(jnp.exp(steps), extent[axis_at] // parts).reshape((-1,) + (1,) * (len(extent) - 1 - axis_at))
    return gain


def shared_out(key, own, number, rows, amount, top, bound, skew):
    order = jax.random.permutation(key, amount)
    packed, common = load_shares(amount, rows * top, bound, skew, True), load_shares(amount, rows * top, bound, skew, False)
    places = jnp.arange(amount)

    def named(tallies, offset_by):
        used = int((tallies > 0).sum())
        fixed = max(1, used // 4)
        moved = fixed + (places - fixed + offset_by * (used - fixed)) % max(1, amount - fixed)
        return jnp.zeros((amount,), jnp.int32).at[order[jnp.where(places < fixed, places, moved)]].set(jnp.asarray(tallies, jnp.int32))

    tallies = jnp.where(number % 4 == 0, named(packed, number // 4), named(common, number - number // 4 - 1))
    mixed = jax.random.permutation(jax.random.fold_in(own, 3), amount)
    source_of, receiver = mixed[0:amount // 2 * 2:2], mixed[1:amount // 2 * 2:2]
    margin = jnp.minimum(tallies[source_of] - 1, bound - tallies[receiver]) // 2
    margin = jnp.where((source_of == order[0]) | (receiver == order[0]) | (tallies[receiver] == 0), 0, jnp.maximum(margin, 0))
    moved = jax.random.randint(jax.random.fold_in(own, 4), (amount // 2,), 0, 1 << 20) % (margin + 1)
    tallies = tallies.at[source_of].add(-moved).at[receiver].add(moved)
    items = jnp.searchsorted(jnp.cumsum(tallies), jnp.arange(rows * top), side="right").astype(jnp.int32)
    table = items.reshape(top, rows).T
    table = table[jax.random.permutation(jax.random.fold_in(own, 1), rows)]
    offset_by = jax.random.randint(jax.random.fold_in(own, 2), (rows, 1), 0, top)
    return jnp.take_along_axis(table, (jnp.arange(top)[None, :] + offset_by) % top, axis=1)


def load_shares(amount, total, bound, lean, full):
    loads = [(1 << 20) // math.isqrt(standing ** lean) + 1 for standing in range(1, amount + 1)]
    largest = bound if full else min(bound, max(-(-total // amount), total * loads[0] // sum(loads)))
    least = 1 if total - largest >= amount - 1 else 0
    counts, rest = [largest] + [least] * (amount - 1), total - largest - least * (amount - 1)
    while rest > 0:
        movable = [i for i in range(1, amount) if counts[i] < largest] or [i for i in range(1, amount) if counts[i] < bound]
        pool, budget = sum([loads[i] for i in movable]), rest
        for i in movable:
            extra = min(bound - counts[i], max(1, budget * loads[i] // pool), rest)
            counts[i] = counts[i] + extra
            rest = rest - extra
    return np.array(counts)


def noise(stream_key, shape, deviation, reach, cuts=(), held_as=jnp.bfloat16):
    values = jax.random.normal(stream_key, shape, jnp.float32) * deviation
    if len(cuts) > 0:
        values = block_scale(stream_key, shape, cuts, -0.22, 0.18) * values
    return jnp.clip(values, min=-reach, max=reach).astype(held_as)


def setup_inputs(seed: int = 0) -> dict:
    key_list = jax.random.split(jax.random.key(seed), 10)
    query = draw_query(jax.random.fold_in(key_list[9], 71), 0)
    key_in = draw_key_in(jax.random.fold_in(key_list[9], 71), 0)
    value = noise(key_list[2], (CLIPS, SEQ, D), 1.0, 6.0, ((0, 8), (1, 16)))
    grad_out = noise(key_list[3], (CLIPS, SEQ, D), 1.0, 6.0, ((0, 8), (1, 16)))
    expert_ids_keys = jax.random.split(jax.random.fold_in(key_list[4], 1), CLIPS * SEQ // TOK)
    expert_ids_turns = jax.random.permutation(jax.random.fold_in(key_list[4], 3), CLIPS * SEQ // TOK)
    expert_ids = jax.vmap(lambda own, number: shared_out(jax.random.fold_in(key_list[4], 2), own, number, TOK, EXPERTS, 2, C, 1))(expert_ids_keys, expert_ids_turns).reshape((CLIPS, SEQ, 2))
    gate_weights = jnp.clip(0.25 + 0.75 * jax.random.uniform(key_list[5], (CLIPS, SEQ, 2), jnp.float32) ** block_scale(key_list[5], (CLIPS, SEQ, 2), ((0, 8), (1, 16)), -0.2, 0.2), 0.25, 1.0)
    w_gate = noise(key_list[6], (EXPERTS, D, FF), D ** -0.5, 0.15625, ((0, 16), (2, 8)))
    w_up = noise(key_list[7], (EXPERTS, D, FF), D ** -0.5, 0.15625, ((0, 16), (2, 8)))
    w_down = noise(key_list[8], (EXPERTS, FF, D), FF ** -0.5, 0.09375, ((0, 16), (1, 8)))
    return {"query": query, "key_in": key_in, "value": value, "grad_out": grad_out, "expert_ids": expert_ids, "gate_weights": gate_weights, "w_gate": w_gate, "w_up": w_up, "w_down": w_down}


def probabilities(qh, kh):
    scores = jnp.dot(qh, kh.T, preferred_element_type=jnp.float32) * (HD ** -0.5)
    top = jnp.max(scores, axis=-1, keepdims=True)
    weights = jnp.exp(scores - top)
    return weights / jnp.sum(weights, axis=-1, keepdims=True)


def head_forward(qh, kh, vh):
    probs = probabilities(qh, kh).astype(jnp.bfloat16)
    return jnp.dot(probs, vh, preferred_element_type=jnp.float32).astype(jnp.bfloat16)


def head_backward(qh, kh, vh, dh):
    probs = probabilities(qh, kh)
    probs_b = probs.astype(jnp.bfloat16)
    dvalue = jnp.dot(probs_b.T, dh, preferred_element_type=jnp.float32).astype(jnp.bfloat16)
    dprobs = jnp.dot(dh, vh.T, preferred_element_type=jnp.float32)
    delta = jnp.sum(probs * dprobs, axis=-1, keepdims=True)
    dscore = (probs * (dprobs - delta) * (HD ** -0.5)).astype(jnp.bfloat16)
    dquery = jnp.dot(dscore, kh, preferred_element_type=jnp.float32).astype(jnp.bfloat16)
    dkey = jnp.dot(dscore.T, qh, preferred_element_type=jnp.float32).astype(jnp.bfloat16)
    return dquery, dkey, dvalue


def expert_core(rows_in, rows_grad, wgate, wup, wdown):
    gate = jnp.dot(rows_in, wgate, preferred_element_type=jnp.float32)
    upper = jnp.dot(rows_in, wup, preferred_element_type=jnp.float32)
    sig = jax.nn.sigmoid(gate)
    silu_gate = gate * sig
    act = (silu_gate * upper).astype(jnp.bfloat16)
    dact = lax.dot_general(rows_grad, wdown, (((1,), (1,)), ((), ())), preferred_element_type=jnp.float32)
    down_grad = lax.dot_general(act, rows_grad, (((0,), (0,)), ((), ())), preferred_element_type=jnp.float32)
    dsilu = sig * (1.0 + gate * (1.0 - sig))
    dgate = (dact * upper * dsilu).astype(jnp.bfloat16)
    dup = (dact * silu_gate).astype(jnp.bfloat16)
    return dgate, dup, down_grad


def slice_partial(dgate, dup, wgate, wup):
    joined = jnp.concatenate([dgate, dup], axis=1)
    weights = jnp.concatenate([wgate, wup], axis=1)
    return lax.dot_general(joined, weights, (((1,), (1,)), ((), ())), preferred_element_type=jnp.float32)


def reference(query, key_in, value, grad_out, expert_ids, gate_weights, w_gate, w_up, w_down):
    clips = query.shape[0]
    seqlen = query.shape[1]
    width = query.shape[2]

    def to_heads(x):
        return x.reshape(clips, seqlen, HEADS, HD).transpose(0, 2, 1, 3).reshape(clips * HEADS, seqlen, HD)

    def from_heads(x):
        return x.reshape(clips, HEADS, seqlen, HD).transpose(0, 2, 1, 3).reshape(clips, seqlen, width)

    qh, kh, vh = to_heads(query), to_heads(key_in), to_heads(value)
    mixed = from_heads(lax.map(lambda t: head_forward(t[0], t[1], t[2]), (qh, kh, vh)))

    blocks = clips * N_SEQ
    routed = 2 * TOK
    ids = expert_ids.reshape(blocks, routed).astype(jnp.int32)
    onehot = (ids[:, :, None] == jnp.arange(EXPERTS, dtype=jnp.int32)[None, None, :]).astype(jnp.int32)
    slots = jnp.sum((jnp.cumsum(onehot, axis=1) - onehot) * onehot, axis=2).astype(jnp.int32)
    block_idx = jnp.broadcast_to(jnp.arange(blocks, dtype=jnp.int32)[:, None], (blocks, routed))
    rows_mixed = jnp.repeat(mixed.reshape(blocks, TOK, width), 2, axis=1)
    scaled = (gate_weights.astype(jnp.float32)[:, :, :, None] * grad_out.astype(jnp.float32)[:, :, None, :]).astype(jnp.bfloat16)
    scaled = scaled.reshape(blocks, routed, width)
    buf_in = jnp.zeros((EXPERTS, blocks, C, width), jnp.bfloat16).at[ids, block_idx, slots].set(rows_mixed)
    buf_grad = jnp.zeros((EXPERTS, blocks, C, width), jnp.bfloat16).at[ids, block_idx, slots].set(scaled)
    share = FF // N_DP

    def one_expert(t):
        rows_in, rows_grad, wgate, wup, wdown = t
        rows_in = rows_in.reshape(blocks * C, width)
        rows_grad = rows_grad.reshape(blocks * C, width)
        dgate, dup, down_grad = expert_core(rows_in, rows_grad, wgate, wup, wdown)
        total = jnp.zeros((blocks * C, width), jnp.float32)
        for j in range(N_DP):
            lo = j * share
            part = slice_partial(dgate[:, lo:lo + share], dup[:, lo:lo + share], wgate[:, lo:lo + share], wup[:, lo:lo + share])
            total = total + part.astype(jnp.bfloat16).astype(jnp.float32)
        return total.astype(jnp.bfloat16).reshape(blocks, C, width), down_grad.astype(jnp.bfloat16)

    row_grad, grad_down = lax.map(one_expert, (buf_in, buf_grad, w_gate, w_up, w_down))
    back = row_grad[ids, block_idx, slots].astype(jnp.float32).reshape(blocks, TOK, 2, width)
    dmixed = grad_out.reshape(blocks, TOK, width).astype(jnp.float32) + back[:, :, 0] + back[:, :, 1]
    dmixed = dmixed.astype(jnp.bfloat16).reshape(clips, seqlen, width)
    dq, dk, dv = lax.map(lambda t: head_backward(t[0], t[1], t[2], t[3]), (qh, kh, vh, to_heads(dmixed)))
    return from_heads(dq), from_heads(dk), from_heads(dv), grad_down
```

```python
import jax
import jax.numpy as jnp
from jax import lax
from jax.experimental import pallas as pl
from jax.experimental.pallas import tpu as pltpu
from jax.sharding import PartitionSpec as P

bf = jnp.bfloat16
f32 = jnp.float32
MESH = pl.DeviceIdType.MESH
HD = 96
SC = HD ** -0.5
C2 = SC * 1.4426950408889634
VLIM = 62 << 20
ORDER = [1, 4, 3, 12, 5, 15, 7, 13, 8, 2, 9, 6, 11, 14, 10]


def nt(a, b):
    return lax.dot_general(a, b, (((1,), (1,)), ((), ())), preferred_element_type=f32)


def nn(a, b):
    return lax.dot_general(a, b, (((1,), (0,)), ((), ())), preferred_element_type=f32)


def tn(a, b):
    return lax.dot_general(a, b, (((0,), (0,)), ((), ())), preferred_element_type=f32)


def iota(shape, dim):
    return lax.broadcasted_iota(jnp.int32, shape, dim)


def onehot(cond):
    return jnp.where(cond, 1.0, 0.0).astype(bf)


class Place:
    def __init__(self):
        self.dp = lax.axis_index("dp")
        self.s = lax.axis_index("seq")
        self.x = self.s // 4
        self.z = lax.rem(self.s, 4)
        self.y = self.dp // 2
        self.core = lax.rem(self.dp, 2)

    def to(self, o):
        dx, dz = o // 4, lax.rem(o, 4) if not isinstance(o, int) else o % 4
        return lax.rem(self.x + dx, 4) * 4 + lax.rem(self.z + dz, 4)

    def source(self, o):
        dx, dz = o // 4, lax.rem(o, 4) if not isinstance(o, int) else o % 4
        return lax.rem(self.x + 4 - dx, 4) * 4 + lax.rem(self.z + 4 - dz, 4)

    def clip(self, k):
        return lax.rem(self.y + k, 4) * 2 + self.core

    def pair(self, k):
        return lax.rem(self.y + k, 4) * 2 + 1 - self.core


def greet(devices):
    b = pltpu.get_barrier_semaphore()
    for d in devices:
        pl.semaphore_signal(b, inc=1, device_id=d, device_id_type=MESH)


def greeted(n):
    pl.semaphore_wait(pltpu.get_barrier_semaphore(), n)


def rcopy(src, dst, ss, rs, dev):
    return pltpu.make_async_remote_copy(
        src_ref=src, dst_ref=dst, send_sem=ss, recv_sem=rs, device_id=dev, device_id_type=MESH
    )


class Exchange:
    def __init__(self, at, send, recv, ss, rs):
        self.at, self.send, self.recv, self.ss, self.rs = at, send, recv, ss, rs

    def out(self, o):
        t = self.at.to(o)
        return rcopy(self.send(t), self.recv(self.at.s), self.ss.at[o], self.rs.at[o], (self.at.dp, t))

    def into(self, o):
        t = self.at.source(o)
        return rcopy(self.send(t), self.recv(t), self.ss.at[o], self.rs.at[o], (self.at.dp, t))

    def start(self):
        for o in ORDER:
            self.out(o).start()

    def wait_recv(self):
        @pl.loop(1, 16)
        def _(o):
            self.into(o).wait_recv()

    def wait_send(self):
        @pl.loop(1, 16)
        def _(o):
            self.out(o).wait_send()


def seq_peers(at):
    return [(at.dp, at.to(o)) for o in ORDER]


def dp_peers(at):
    return [(at.clip(1), at.s), (at.clip(3), at.s), (at.clip(2), at.s), (at.pair(0), at.s)]


def main_places(M, b):
    io = iota((256, 128), 0).astype(f32)
    return onehot((io == M[b, 0:1, :]) | (io == M[b, 1:2, :]))


def extra_places(M, b):
    io = iota((512, 128), 0)
    low = lax.rem(io, 32)
    own = (low // 2) == b
    tgt = ((io // 32) * 2 + lax.rem(io, 2)).astype(f32)
    return onehot(own & ((tgt == M[b, 2:3, :]) | (tgt == M[b, 3:4, :])))


class Gather:
    def __init__(self, at, buf, ss, rs):
        self.at, self.buf, self.ss, self.rs = at, buf, ss, rs

    def half(self, c, i):
        return self.buf.at[c, pl.ds(144 * i, 144), :]

    def copy(self, n, c, i, dev):
        ref = self.half(c, i)
        return rcopy(ref, ref, self.ss.at[n], self.rs.at[n], (dev, self.at.s))

    def own_out(self):
        a = self.at
        for i in (0, 1):
            self.copy(i, a.clip(0), i, a.clip(1)).start()
            self.copy(2 + 1 - i, a.clip(0), 1 - i, a.clip(3)).start()
        for i in (0, 1):
            self.copy(6 + i, a.clip(0), i, a.pair(0)).start()

    def relay(self):
        a = self.at
        self.copy(0, a.clip(3), 0, a.clip(1)).wait_recv()
        self.copy(4, a.clip(3), 0, a.clip(1)).start()
        self.copy(8, a.clip(3), 0, a.pair(0)).start()
        self.copy(3, a.clip(1), 1, a.clip(3)).wait_recv()
        self.copy(5, a.clip(1), 1, a.clip(3)).start()
        self.copy(11, a.clip(1), 1, a.pair(0)).start()

    def rest(self):
        a = self.at
        self.copy(1, a.clip(3), 1, a.clip(1)).wait_recv()
        self.copy(9, a.clip(3), 1, a.pair(0)).start()
        self.copy(2, a.clip(1), 0, a.clip(3)).wait_recv()
        self.copy(10, a.clip(1), 0, a.pair(0)).start()

    def far(self):
        a = self.at
        self.copy(4, a.clip(2), 0, a.clip(1)).wait_recv()
        self.copy(12, a.clip(2), 0, a.pair(0)).start()
        self.copy(5, a.clip(2), 1, a.clip(3)).wait_recv()
        self.copy(13, a.clip(2), 1, a.pair(0)).start()

    def other(self, k):
        n = {0: 6, 3: 8, 1: 10, 2: 12}[k]
        for i in (0, 1):
            self.copy(n + i, self.at.pair(k), i, self.at.pair(0)).wait_recv()

    def wait_send(self):
        for n in range(14):
            self.copy(n, self.at.clip(0), 0, self.at.clip(1)).wait_send()


def attention(j, Q, K, Vt, ET, Oa, mixed, s_ref):
    CH = 512
    q0 = pl.multiple_of(j * 256, 256)
    Qj = Q[pl.ds(q0, 256), :]
    m = None
    for c in range(2048 // CH):
        s = nt(K[c * CH:(c + 1) * CH, :], Qj)
        s_ref[c * CH:(c + 1) * CH, :] = s
        mc = jnp.max(s.reshape(CH // 8, 8, 256), axis=0)
        m = mc if m is None else jnp.maximum(m, mc)
    m = jnp.max(m, axis=0, keepdims=True) * C2
    for c in range(2048 // CH):
        e = jnp.exp2(s_ref[c * CH:(c + 1) * CH, :] * C2 - m).astype(bf)
        ET[c * CH:(c + 1) * CH, pl.ds(q0, 256)] = e
    ot = nn(Vt[...], ET[:, pl.ds(q0, 256)])
    linv = 1.0 / ot[96:97, :]
    on = jnp.concatenate([ot[:96, :] * linv, jnp.broadcast_to(linv, (32, 256))], axis=0)
    o = on.T
    Oa[pl.ds(q0, 256), :] = o
    mixed[pl.ds(q0, 256), :] = o.astype(bf)


def front(q, k, v, go, meta, Q, K, V, G, ET, Oa, M, rows, SA,
          Sx, Rx, Ms, SM, RM, SX, RX, B, RB, Vt, mixed, s_ref,
          ss_x, rs_x, ss_m, rs_m, ss_s, rs_s, ss_e, rs_e, ss_b, rs_b, ss_g, rs_g):
    at = Place()
    greet(seq_peers(at) + dp_peers(at))

    e0, e1, g0, g1 = (meta[i:i + 1, :] for i in range(4))
    ie = iota((16, 128), 0).astype(f32)
    oh0, oh1 = jnp.where(ie == e0, 1.0, 0.0), jnp.where(ie == e1, 1.0, 0.0)
    before = onehot(iota((128, 128), 0) < iota((128, 128), 1))
    count = nn((oh0 + oh1).astype(bf), before)
    s0 = jnp.sum(oh0 * count, axis=0, keepdims=True)
    s1 = jnp.sum(oh1 * count, axis=0, keepdims=True)
    m0 = jnp.where(s0 < 16, e0 * 16 + s0, -1.0)
    m1 = jnp.where(s1 < 16, e1 * 16 + s1, -1.0)
    x0 = jnp.where(s0 < 16, -1.0, e0 * 2 + s0 - 16)
    x1 = jnp.where(s1 < 16, -1.0, e1 * 2 + s1 - 16)
    Ms[...] = jnp.concatenate([m0, m1, x0, x1, m0, m0, m0, m0], axis=0)

    io = iota((256, 128), 0).astype(f32)
    c0, c1 = io == m0, io == m1
    gw = jnp.sum(jnp.where(c0, g0, 0.0) + jnp.where(c1, g1, 0.0), axis=1, keepdims=True)
    pm = onehot(c0 | c1)
    for n in range(3):
        cols = slice(512 * n, 512 * n + 512)
        SM[:, :, cols] = (nn(pm, go[:, cols]) * gw).astype(bf).reshape(16, 16, 512)
    io = iota((32, 128), 0).astype(f32)
    c0, c1 = io == x0, io == x1
    gw = jnp.sum(jnp.where(c0, g0, 0.0) + jnp.where(c1, g1, 0.0), axis=1, keepdims=True)
    ext = (nn(onehot(c0 | c1), go[...]) * gw).astype(bf)
    stack = jnp.concatenate([ext[:, 128 * g:128 * g + 128] for g in range(12)], axis=0)
    r, c = iota((512, 384), 0), iota((512, 384), 1)
    low = lax.rem(r, 32)
    spread = onehot(c == (low // 2) * 32 + (r // 32) * 2 + lax.rem(low, 2))
    SX[...] = nn(spread, stack).astype(bf).reshape(16, 32, 128)

    for n, ref in enumerate((q, k, v, go)):
        for h in range(16):
            Sx[n, h] = jnp.concatenate(
                [ref[32 * g:32 * g + 32, 96 * h:96 * h + 96] for g in range(4)], axis=1)

    greeted(19)
    xm = Exchange(at, lambda t: Ms, lambda t: M.at[t], ss_m, rs_m)
    xs = Exchange(at, lambda t: SM.at[t], lambda t: RM.at[t], ss_s, rs_s)
    xe = Exchange(at, lambda t: SX.at[t], lambda t: RX.at[t], ss_e, rs_e)
    xq = [Exchange(at, lambda t, n=n: Sx.at[n, t], lambda t, n=n: Rx.at[n, t], ss_x.at[n], rs_x.at[n])
          for n in range(4)]
    xs.start()
    xe.start()
    for n in range(4):
        xq[n].start()
    xm.start()
    M[at.s] = Ms[...]
    RM[at.s] = SM[at.s]
    RX[at.s] = SX[at.s]
    for n in range(4):
        Rx[n, at.s] = Sx[n, at.s]

    xs.wait_recv()
    SA[at.dp, 0:256, :] = RM[...].reshape(256, 1536)
    xe.wait_recv()
    r, c = iota((384, 512), 1), iota((384, 512), 0)
    low = lax.rem(r, 32)
    pick = onehot(c == (low // 2) * 32 + (r // 32) * 2 + lax.rem(low, 2))
    back = nn(pick, RX[...].reshape(512, 128)).astype(bf)
    SA[at.dp, 256:288, :] = jnp.concatenate([back[32 * g:32 * g + 32] for g in range(12)], axis=1)
    ga = Gather(at, SA, ss_g, rs_g)
    ga.own_out()

    def unpack(n, dst, fill):
        @pl.loop(0, 16)
        def _(b):
            w = Rx[n, b]
            for g in range(4):
                dst[pl.ds(pl.multiple_of(b * 128 + 32 * g, 32), 32), :] = jnp.concatenate(
                    [w[:, 96 * g:96 * g + 96], jnp.full((32, 32), fill, bf)], axis=1)

    for n, dst, fill in ((0, Q, 0), (1, K, 0), (2, V, 1)):
        xq[n].wait_recv()
        unpack(n, dst, fill)
    Vt[...] = V[...].T
    xm.wait_recv()

    xb = []
    for half in (0, 1):
        @pl.loop(4 * half, 4 * half + 4)
        def _(j):
            attention(j, Q, K, Vt, ET, Oa, mixed, s_ref)
        if half == 0:
            ga.relay()
        for j in range(4 * half, 4 * half + 4):
            for i in (0, 1):
                b = 2 * j + i
                w = nn(main_places(M, b), mixed[128 * b:128 * b + 128, :]).astype(bf)
                B[:, 16 * i:16 * i + 16, 96 * j:96 * j + 96] = w[:, :96].reshape(16, 16, 96)
        cols = pl.ds(384 * half, 384)
        xb.append(Exchange(at, lambda t, cols=cols: B.at[t, :, cols], lambda t, cols=cols: RB.at[t, :, cols],
                           ss_b.at[half], rs_b.at[half]))
        xb[half].start()
    acc = jnp.zeros((512, 128), f32)
    for b in range(16):
        acc = acc + nn(extra_places(M, b), mixed[128 * b:128 * b + 128, :])
    B[:, :, 768:864] = acc[:, :96].astype(bf).reshape(16, 32, 96)
    B[:, :, 864:896] = jnp.zeros((16, 32, 32), bf)
    cols = pl.ds(768, 128)
    xb.append(Exchange(at, lambda t: B.at[t, :, cols], lambda t: RB.at[t, :, cols], ss_b.at[2], rs_b.at[2]))
    xb[2].start()
    RB[at.s] = B[at.s]
    ga.rest()
    xq[3].wait_recv()
    unpack(3, G, 0)

    for part in range(3):
        xb[part].wait_recv()
        for j in range(4 * part, min(4 * part + 4, 9)):
            rows[32 * j:32 * j + 32, :] = jnp.concatenate(
                [RB[h, :, 96 * j:96 * j + 96] for h in range(16)], axis=1)
    ga.far()
    for kk in range(4):
        ga.other(kk)
    for e in [xm, xs, xe] + xq + xb:
        e.wait_send()
    ga.wait_send()


def expert(rows, SA, wg, wu, wd, own_sum, grad_down, RA, ACT, DG, PT, SR, SS, RR,
           ss_g, rs_g, ss_s, rs_s, ss_r, rs_r):
    at = Place()
    greet(dp_peers(at))
    RA[at.dp] = rows[...]
    greeted(4)
    ga = Gather(at, RA, ss_g, rs_g)
    ga.own_out()

    def chunk(c):
        X = RA[c]
        Gr = SA[c]
        for f in range(2):
            fs = slice(256 * f, 256 * f + 256)
            gate = nn(X, wg[:, fs])
            up = nn(X, wu[:, fs])
            dact = nt(Gr, wd[fs, :])
            sig = 1.0 / (1.0 + jnp.exp(-gate))
            silu = gate * sig
            ACT[c, :, fs] = (silu * up).astype(bf)
            DG[:, 256 * f:256 * f + 256] = (dact * up * (sig * (1.0 + gate * (1.0 - sig)))).astype(bf)
            DG[:, 512 + 256 * f:768 + 256 * f] = (dact * silu).astype(bf)
        for n in range(3):
            ns = slice(512 * n, 512 * n + 512)
            PT[c, :, ns] = (nt(DG[:, :512], wg[ns, :]) + nt(DG[:, 512:], wu[ns, :])).astype(bf)

    def sib(k):
        return rcopy(PT.at[at.pair(k)], SR.at[k], ss_s.at[k], rs_s.at[k], (at.pair(0), at.s))

    def out(k):
        return rcopy(SS.at[k], RR.at[k], ss_r.at[k], rs_r.at[k], (at.clip(k), at.s))

    def send(k):
        sib(k).wait_recv()
        SS[k] = (PT[at.clip(k)].astype(f32) + SR[k].astype(f32)).astype(bf)
        if k:
            out(k).start()

    def work(k):
        chunk(at.pair(k))
        sib(k).start()
        chunk(at.clip(k))

    ga.other(0)
    work(0)
    ga.relay()
    ga.rest()
    send(0)
    ga.other(1)
    work(1)
    send(1)
    ga.far()
    ga.other(3)
    work(3)
    send(3)
    ga.other(2)
    work(2)
    send(2)
    for n in range(3):
        ns = slice(512 * n, 512 * n + 512)
        grad_down[:, ns] = tn(ACT[...].reshape(2304, 512), SA[:, :, ns].reshape(2304, 512)).astype(bf)
    total = SS[0].astype(f32)
    for k in (1, 3, 2):
        out(k).wait_recv()
        total = total + RR[k].astype(f32)
    own_sum[...] = total.astype(bf)
    for k in range(4):
        sib(k).wait_send()
        if k:
            out(k).wait_send()
    ga.wait_send()


def attention_back(j, dO, V, Kt, ET, Oa, dST, dOs, dQ):
    CH = 512
    q0 = pl.multiple_of(j * 256, 256)
    d = dO[pl.ds(q0, 256), :96].astype(f32)
    oa = Oa[pl.ds(q0, 256), :]
    linv = oa[:, 96:97]
    delta = -jnp.sum(d * oa[:, :96], axis=1, keepdims=True)
    hi = delta.astype(bf)
    r = delta - hi.astype(f32)
    mid = r.astype(bf)
    lo = (r - mid.astype(f32)).astype(bf)
    daug = jnp.concatenate([d.astype(bf), hi, mid, lo, jnp.zeros((256, 29), bf)], axis=1)
    dOs[pl.ds(q0, 256), :] = jnp.concatenate([(d * linv).astype(bf), jnp.zeros((256, 32), bf)], axis=1)
    for c in range(2048 // CH):
        dp = nt(V[c * CH:(c + 1) * CH, :], daug).astype(bf)
        dST[c * CH:(c + 1) * CH, pl.ds(q0, 256)] = ET[c * CH:(c + 1) * CH, pl.ds(q0, 256)] * dp
    dqt = nn(Kt[...], dST[:, pl.ds(q0, 256)])
    dQ[pl.ds(q0, 256), :] = (dqt.T * (linv * SC)).astype(bf)


def finish(total, Q, K, V, G, ET, Oa, M, gq, gk, gv,
           B, RB, dO, Kt, dST, dOs, Qs, dX, So, Ro, ss_b, rs_b, ss_o, rs_o):
    at = Place()
    greet(seq_peers(at))
    xb = []
    for part in range(3):
        cols = pl.ds(384 * part, 384 if part < 2 else 128)
        xb.append(Exchange(at, lambda t, cols=cols: B.at[t, :, cols], lambda t, cols=cols: RB.at[t, :, cols],
                           ss_b.at[part], rs_b.at[part]))
    for part in range(3):
        for h in range(16):
            parts = [total[32 * j:32 * j + 32, 96 * h:96 * h + 96] for j in range(4 * part, min(4 * part + 4, 9))]
            if part == 2:
                parts.append(jnp.zeros((32, 32), bf))
            B[h, :, 384 * part:384 * part + (384 if part < 2 else 128)] = jnp.concatenate(parts, axis=1)
        if part == 0:
            greeted(15)
        xb[part].start()
    RB[at.s] = B[at.s]
    Kt[...] = K[...].T
    Qs[...] = (Q[...].astype(f32) * (Oa[:, 96:97] * SC)).astype(bf)
    xb[2].wait_recv()
    extra = RB[:, :, 768:896].reshape(512, 128)
    for part in range(2):
        xb[part].wait_recv()
        for j in range(4 * part, 4 * part + 4):
            for i in (0, 1):
                b = 2 * j + i
                w = RB[:, 16 * i:16 * i + 16, 96 * j:96 * j + 96].reshape(256, 96)
                t = slice(128 * b, 128 * b + 128)
                dm = tn(main_places(M, b), w) + tn(extra_places(M, b), extra)[:, :96] + G[t, :96].astype(f32)
                dO[t, :96] = dm.astype(bf)

    xo = [Exchange(at, lambda t, n=n: So.at[n, t], lambda t, n=n: Ro.at[n, t], ss_o.at[n], rs_o.at[n])
          for n in range(3)]

    def pack(n):
        @pl.loop(0, 16)
        def _(b):
            So[n, b] = jnp.concatenate(
                [dX[pl.ds(pl.multiple_of(b * 128 + 32 * g, 32), 32), :96] for g in range(4)], axis=1)
        Ro[n, at.s] = So[n, at.s]
        xo[n].start()

    @pl.loop(0, 8)
    def _(j):
        attention_back(j, dO, V, Kt, ET, Oa, dST, dOs, dX)
    pack(0)
    for n, a, b in ((1, dST, Qs), (2, ET, dOs)):
        @pl.loop(0, 4)
        def _(i):
            r = pl.ds(pl.multiple_of(i * 512, 512), 512)
            dX[r, :] = nn(a[r, :], b[...]).astype(bf)
        pack(n)
    for n, dst in enumerate((gq, gk, gv)):
        xo[n].wait_recv()
        for g in range(4):
            dst[32 * g:32 * g + 32, :] = jnp.concatenate(
                [Ro[n, h, :, 96 * g:96 * g + 96] for h in range(16)], axis=1)
    for e in xb + xo:
        e.wait_send()


def call(kernel, outs, scratch, cid, *args):
    return pl.pallas_call(
        kernel,
        out_shape=[jax.ShapeDtypeStruct(s, d) for s, d in outs],
        scratch_shapes=scratch,
        name=kernel.__name__,
        compiler_params=pltpu.CompilerParams(collective_id=cid, has_side_effects=True, vmem_limit_bytes=VLIM),
    )(*args)


def vm(*shape, dtype=bf):
    return pltpu.VMEM(shape, dtype)


def dma(*shape):
    return pltpu.SemaphoreType.DMA(shape)


def run_front(query, key_in, value, grad_out, expert_ids, gate_weights):
    ids = expert_ids[0].astype(f32).T
    meta = jnp.concatenate([ids, gate_weights[0].T, jnp.zeros((4, 128), f32)], axis=0)
    return call(
        front,
        [((2048, 128), bf)] * 4 + [((2048, 2048), bf), ((2048, 128), f32), ((16, 8, 128), f32),
                                   ((288, 1536), bf), ((8, 288, 1536), bf)],
        [vm(4, 16, 32, 384), vm(4, 16, 32, 384), vm(8, 128, dtype=f32), vm(16, 16, 1536), vm(16, 16, 1536),
         vm(16, 32, 128), vm(16, 32, 128), vm(16, 32, 896), vm(16, 32, 896), vm(128, 2048), vm(2048, 128),
         vm(2048, 256, dtype=f32)]
        + [dma(4, 16)] * 2 + [dma(16)] * 6 + [dma(3, 16)] * 2 + [dma(14)] * 2,
        0, query[0], key_in[0], value[0], grad_out[0], meta)


def per_device(query, key_in, value, grad_out, expert_ids, gate_weights, w_gate, w_up, w_down):
    Q, K, V, G, ET, Oa, M, rows, SA = run_front(query, key_in, value, grad_out, expert_ids, gate_weights)
    total, grad_down = call(
        expert,
        [((288, 1536), bf), ((512, 1536), bf)],
        [vm(8, 288, 1536), vm(8, 288, 512), vm(288, 1024), vm(8, 288, 1536), vm(4, 288, 1536), vm(4, 288, 1536),
         vm(4, 288, 1536)] + [dma(14)] * 2 + [dma(4)] * 4,
        1, rows, SA, w_gate[0], w_up[0], w_down[0])
    gq, gk, gv = call(
        finish,
        [((128, 1536), bf)] * 3,
        [vm(16, 32, 896), vm(16, 32, 896), vm(2048, 128), vm(128, 2048), vm(2048, 2048), vm(2048, 128),
         vm(2048, 128), vm(2048, 128), vm(3, 16, 32, 384), vm(3, 16, 32, 384)]
        + [dma(3, 16)] * 4,
        2, total, Q, K, V, G, ET, Oa, M)
    return (gq[None], gk[None], gv[None], grad_down[None])


def solution(mesh):
    seq = P("dp", "seq", None)
    return jax.shard_map(
        per_device,
        mesh=mesh,
        in_specs=(seq,) * 6 + (P("seq", None, "dp"), P("seq", None, "dp"), P("seq", "dp", None)),
        out_specs=(seq, seq, seq, P("seq", "dp", None)),
        check_vma=False,
    )
```

```python
import jax
import jax.numpy as jnp
from jax import lax
from jax.experimental import pallas as pl
from jax.experimental.pallas import tpu as pltpu
from jax.sharding import PartitionSpec as P

bf = jnp.bfloat16
f32 = jnp.float32
MESH = pl.DeviceIdType.MESH
HD = 96
SC = HD ** -0.5
C2 = SC * 1.4426950408889634
VLIM = 62 << 20
ORDER = [1, 4, 3, 12, 5, 15, 7, 13, 8, 2, 9, 6, 11, 14, 10]


def nt(a, b):
    return lax.dot_general(a, b, (((1,), (1,)), ((), ())), preferred_element_type=f32)


def nn(a, b):
    return lax.dot_general(a, b, (((1,), (0,)), ((), ())), preferred_element_type=f32)


def tn(a, b):
    return lax.dot_general(a, b, (((0,), (0,)), ((), ())), preferred_element_type=f32)


def iota(shape, dim):
    return lax.broadcasted_iota(jnp.int32, shape, dim)


def onehot(cond):
    return jnp.where(cond, 1.0, 0.0).astype(bf)


class Place:
    def __init__(self):
        self.dp = lax.axis_index("dp")
        self.s = lax.axis_index("seq")
        self.x = self.s // 4
        self.z = lax.rem(self.s, 4)
        self.y = self.dp // 2
        self.core = lax.rem(self.dp, 2)

    def to(self, o):
        dx, dz = o // 4, lax.rem(o, 4) if not isinstance(o, int) else o % 4
        return lax.rem(self.x + dx, 4) * 4 + lax.rem(self.z + dz, 4)

    def source(self, o):
        dx, dz = o // 4, lax.rem(o, 4) if not isinstance(o, int) else o % 4
        return lax.rem(self.x + 4 - dx, 4) * 4 + lax.rem(self.z + 4 - dz, 4)

    def clip(self, k):
        return lax.rem(self.y + k, 4) * 2 + self.core

    def pair(self, k):
        return lax.rem(self.y + k, 4) * 2 + 1 - self.core


def greet(devices):
    b = pltpu.get_barrier_semaphore()
    for d in devices:
        pl.semaphore_signal(b, inc=1, device_id=d, device_id_type=MESH)


def greeted(n):
    pl.semaphore_wait(pltpu.get_barrier_semaphore(), n)


def rcopy(src, dst, ss, rs, dev):
    return pltpu.make_async_remote_copy(
        src_ref=src, dst_ref=dst, send_sem=ss, recv_sem=rs, device_id=dev, device_id_type=MESH
    )


class Exchange:
    def __init__(self, at, send, recv, ss, rs):
        self.at, self.send, self.recv, self.ss, self.rs = at, send, recv, ss, rs

    def out(self, o):
        t = self.at.to(o)
        return rcopy(self.send(t), self.recv(self.at.s), self.ss.at[o], self.rs.at[o], (self.at.dp, t))

    def into(self, o):
        t = self.at.source(o)
        return rcopy(self.send(t), self.recv(t), self.ss.at[o], self.rs.at[o], (self.at.dp, t))

    def start(self):
        for o in ORDER:
            self.out(o).start()

    def wait_recv(self):
        @pl.loop(1, 16)
        def _(o):
            self.into(o).wait_recv()

    def wait_send(self):
        @pl.loop(1, 16)
        def _(o):
            self.out(o).wait_send()


def seq_peers(at):
    return [(at.dp, at.to(o)) for o in ORDER]


def dp_peers(at):
    return [(at.clip(1), at.s), (at.clip(3), at.s), (at.clip(2), at.s), (at.pair(0), at.s)]


def main_places(M, b):
    io = iota((256, 128), 0).astype(f32)
    return onehot((io == M[b, 0:1, :]) | (io == M[b, 1:2, :]))


def extra_places(M, b):
    io = iota((512, 128), 0)
    low = lax.rem(io, 32)
    own = (low // 2) == b
    tgt = ((io // 32) * 2 + lax.rem(io, 2)).astype(f32)
    return onehot(own & ((tgt == M[b, 2:3, :]) | (tgt == M[b, 3:4, :])))


class Gather:
    def __init__(self, at, buf, base, ss, rs):
        self.at, self.buf, self.base, self.ss, self.rs = at, buf, base, ss, rs

    def half(self, c, i):
        return self.buf.at[self.base + c, pl.ds(144 * i, 144), :]

    def copy(self, n, c, i, dev):
        ref = self.half(c, i)
        return rcopy(ref, ref, self.ss.at[n], self.rs.at[n], (dev, self.at.s))

    def own_out(self):
        a = self.at
        for i in (0, 1):
            self.copy(i, a.clip(0), i, a.clip(1)).start()
            self.copy(2 + 1 - i, a.clip(0), 1 - i, a.clip(3)).start()
        for i in (0, 1):
            self.copy(6 + i, a.clip(0), i, a.pair(0)).start()

    def relay(self):
        a = self.at
        self.copy(0, a.clip(3), 0, a.clip(1)).wait_recv()
        self.copy(4, a.clip(3), 0, a.clip(1)).start()
        self.copy(8, a.clip(3), 0, a.pair(0)).start()
        self.copy(3, a.clip(1), 1, a.clip(3)).wait_recv()
        self.copy(5, a.clip(1), 1, a.clip(3)).start()
        self.copy(11, a.clip(1), 1, a.pair(0)).start()

    def rest(self):
        a = self.at
        self.copy(1, a.clip(3), 1, a.clip(1)).wait_recv()
        self.copy(9, a.clip(3), 1, a.pair(0)).start()
        self.copy(2, a.clip(1), 0, a.clip(3)).wait_recv()
        self.copy(10, a.clip(1), 0, a.pair(0)).start()

    def far(self):
        a = self.at
        self.copy(4, a.clip(2), 0, a.clip(1)).wait_recv()
        self.copy(12, a.clip(2), 0, a.pair(0)).start()
        self.copy(5, a.clip(2), 1, a.clip(3)).wait_recv()
        self.copy(13, a.clip(2), 1, a.pair(0)).start()

    def other(self, k):
        n = {0: 6, 3: 8, 1: 10, 2: 12}[k]
        for i in (0, 1):
            self.copy(n + i, self.at.pair(k), i, self.at.pair(0)).wait_recv()

    def wait_send(self):
        for n in range(14):
            self.copy(n, self.at.clip(0), 0, self.at.clip(1)).wait_send()


def scores(j, Q, K, ET, s_ref):
    CH = 512
    q0 = pl.multiple_of(j * 256, 256)
    Qj = Q[pl.ds(q0, 256), :]
    m = None
    for c in range(2048 // CH):
        s = nt(K[c * CH:(c + 1) * CH, :], Qj)
        s_ref[c * CH:(c + 1) * CH, :] = s
        mc = jnp.max(s.reshape(CH // 8, 8, 256), axis=0)
        m = mc if m is None else jnp.maximum(m, mc)
    m = jnp.max(m, axis=0, keepdims=True) * C2
    for c in range(2048 // CH):
        e = jnp.exp2(s_ref[c * CH:(c + 1) * CH, :] * C2 - m).astype(bf)
        ET[c * CH:(c + 1) * CH, pl.ds(q0, 256)] = e


def mix(j, Vt, ET, Oa, mixed):
    q0 = pl.multiple_of(j * 256, 256)
    ot = nn(Vt[...], ET[:, pl.ds(q0, 256)])
    linv = 1.0 / ot[96:97, :]
    on = jnp.concatenate([ot[:96, :] * linv, jnp.broadcast_to(linv, (32, 256))], axis=0)
    o = on.T
    Oa[pl.ds(q0, 256), :] = o
    mixed[pl.ds(q0, 256), :] = o.astype(bf)


def scale_back(dO, Oa, dOs):
    @pl.loop(0, 8)
    def _(j):
        r = pl.ds(pl.multiple_of(j * 256, 256), 256)
        dOs[r, :] = (dO[r, :].astype(f32) * Oa[r, 96:97]).astype(bf)


def dscore_at(j, kb):
    if j < 6:
        return kb, 256 * j
    return 8 + kb // 3, 512 * (kb % 3) + 256 * (j - 6)


def dscores(j, dO, V, Kt, ET, Oa, AG, dX):
    r = slice(256 * j, 256 * j + 256)
    d = dO[r, :96].astype(f32)
    oa = Oa[r, :]
    delta = -jnp.sum(d * oa[:, :96], axis=1, keepdims=True)
    hi = delta.astype(bf)
    rest = delta - hi.astype(f32)
    mid = rest.astype(bf)
    lo = (rest - mid.astype(f32)).astype(bf)
    daug = jnp.concatenate([d.astype(bf), hi, mid, lo, jnp.zeros((256, 29), bf)], axis=1)
    dqt = None
    for kb in range(8):
        ks = slice(256 * kb, 256 * kb + 256)
        ds = ET[ks, r] * nt(V[ks, :], daug).astype(bf)
        slot, lane = dscore_at(j, kb)
        AG[slot, 0:256, lane:lane + 256] = ds
        term = nn(Kt[:, ks], ds)
        dqt = term if dqt is None else dqt + term
    dX[r, :] = (dqt.T * (oa[:, 96:97] * SC)).astype(bf)


def block(q, k, v, go, ids, gws, wg_hbm, wu_hbm, wd_hbm, R, grad_down,
          S, SG, RG, Ms, M, SM, RM, SX, RX, B, RB, RB2, wg, wu, wd, AG, ET, Q, K, V, T, X, Qs, Oa, s_ref,
          ACT, DG, PT, SR, SS, RR,
          ss_x, rs_x, ss_y, rs_y, ss_m, rs_m, ss_s, rs_s, ss_e, rs_e, ss_b, rs_b, ss_c, rs_c, ss_g, rs_g, ss_h, rs_h,
          ss_p, rs_p, ss_r, rs_r, sem_w):
    at = Place()
    greet(seq_peers(at) + dp_peers(at))
    weights = [pltpu.make_async_copy(a, b, sem_w.at[n])
               for n, (a, b) in enumerate(((wg_hbm, wg), (wu_hbm, wu), (wd_hbm, wd)))]

    e0, e1 = ids[0:1, :].astype(f32), ids[1:2, :].astype(f32)
    g0, g1 = gws[0:1, :], gws[1:2, :]
    ie = iota((16, 128), 0).astype(f32)
    oh0, oh1 = jnp.where(ie == e0, 1.0, 0.0), jnp.where(ie == e1, 1.0, 0.0)
    before = onehot(iota((128, 128), 0) < iota((128, 128), 1))
    count = nn((oh0 + oh1).astype(bf), before)
    s0 = jnp.sum(oh0 * count, axis=0, keepdims=True)
    s1 = jnp.sum(oh1 * count, axis=0, keepdims=True)
    m0 = jnp.where(s0 < 16, e0 * 16 + s0, -1.0)
    m1 = jnp.where(s1 < 16, e1 * 16 + s1, -1.0)
    x0 = jnp.where(s0 < 16, -1.0, e0 * 2 + s0 - 16)
    x1 = jnp.where(s1 < 16, -1.0, e1 * 2 + s1 - 16)
    Ms[...] = jnp.concatenate([m0, m1, x0, x1, m0, m0, m0, m0], axis=0)

    io = iota((256, 128), 0).astype(f32)
    c0, c1 = io == m0, io == m1
    gw = jnp.sum(jnp.where(c0, g0, 0.0) + jnp.where(c1, g1, 0.0), axis=1, keepdims=True)
    pm = onehot(c0 | c1)
    for n in range(3):
        cols = slice(512 * n, 512 * n + 512)
        SM[:, :, cols] = (nn(pm, go[:, cols]) * gw).astype(bf).reshape(16, 16, 512)
    io = iota((32, 128), 0).astype(f32)
    c0, c1 = io == x0, io == x1
    gw = jnp.sum(jnp.where(c0, g0, 0.0) + jnp.where(c1, g1, 0.0), axis=1, keepdims=True)
    ext = (nn(onehot(c0 | c1), go[...]) * gw).astype(bf)
    stack = jnp.concatenate([ext[:, 128 * g:128 * g + 128] for g in range(12)], axis=0)
    r, c = iota((512, 384), 0), iota((512, 384), 1)
    low = lax.rem(r, 32)
    spread = onehot(c == (low // 2) * 32 + (r // 32) * 2 + lax.rem(low, 2))
    SX[...] = nn(spread, stack).astype(bf).reshape(16, 32, 128)

    xm = Exchange(at, lambda t: Ms, lambda t: M.at[t], ss_m, rs_m)
    xs = Exchange(at, lambda t: SM.at[t], lambda t: RM.at[t], ss_s, rs_s)
    xe = Exchange(at, lambda t: SX.at[t], lambda t: RX.at[t], ss_e, rs_e)
    xq = [Exchange(at, lambda t, n=n: S.at[n, t], lambda t, n=n: R.at[n, t], ss_x.at[n], rs_x.at[n])
          for n in range(3)]
    xg = Exchange(at, lambda t: SG.at[t], lambda t: RG.at[t], ss_x.at[3], rs_x.at[3])

    def pack(ref, put):
        for h in range(16):
            put(h, jnp.concatenate(
                [ref[32 * g:32 * g + 32, 96 * h:96 * h + 96] for g in range(4)], axis=1))

    greeted(19)
    xs.start()
    xe.start()
    for n, ref in ((1, k), (0, q), (2, v)):
        def put(h, w):
            S[n, h] = w
        pack(ref, put)
        R[n, at.s] = S[n, at.s]
        xq[n].start()
    xm.start()

    def put_g(h, w):
        SG[h] = w
    pack(go, put_g)
    RG[at.s] = SG[at.s]
    xg.start()
    for w in weights:
        w.start()
    M[at.s] = Ms[...]
    RM[at.s] = SM[at.s]
    RX[at.s] = SX[at.s]

    xs.wait_recv()
    AG[at.dp, 0:256, :] = RM[...].reshape(256, 1536)
    xe.wait_recv()
    r, c = iota((384, 512), 1), iota((384, 512), 0)
    low = lax.rem(r, 32)
    pick = onehot(c == (low // 2) * 32 + (r // 32) * 2 + lax.rem(low, 2))
    back = nn(pick, RX[...].reshape(512, 128)).astype(bf)
    AG[at.dp, 256:288, :] = jnp.concatenate([back[32 * g:32 * g + 32] for g in range(12)], axis=1)
    gs = Gather(at, AG, 0, ss_g, rs_g)
    gs.own_out()

    def unpack(n, dst, fill):
        @pl.loop(0, 16)
        def _(b):
            w = R[n, b]
            for g in range(4):
                dst[pl.ds(pl.multiple_of(b * 128 + 32 * g, 32), 32), :] = jnp.concatenate(
                    [w[:, 96 * g:96 * g + 96], jnp.full((32, 32), fill, bf)], axis=1)

    xq[1].wait_recv()
    unpack(1, K, 0)
    xq[0].wait_recv()
    unpack(0, Q, 0)

    @pl.loop(0, 8)
    def _(j):
        scores(j, Q, K, ET, s_ref)
    gs.relay()
    xq[2].wait_recv()
    unpack(2, V, 1)
    T[...] = V[...].T
    xm.wait_recv()

    xb = []
    for part in range(3):
        cols = pl.ds(384 * part, 384 if part < 2 else 128)
        xb.append(Exchange(at, lambda t, cols=cols: B.at[t, :, cols], lambda t, cols=cols: RB.at[t, :, cols],
                           ss_b.at[part], rs_b.at[part]))
    for part in (0, 1):
        @pl.loop(4 * part, 4 * part + 4)
        def _(j):
            mix(j, T, ET, Oa, X)
        for j in range(4 * part, 4 * part + 4):
            for i in (0, 1):
                b = 2 * j + i
                w = nn(main_places(M, b), X[128 * b:128 * b + 128, :]).astype(bf)
                B[:, 16 * i:16 * i + 16, 96 * j:96 * j + 96] = w[:, :96].reshape(16, 16, 96)
        xb[part].start()
    acc = jnp.zeros((512, 128), f32)
    for b in range(16):
        acc = acc + nn(extra_places(M, b), X[128 * b:128 * b + 128, :])
    B[:, :, 768:864] = acc[:, :96].astype(bf).reshape(16, 32, 96)
    B[:, :, 864:896] = jnp.zeros((16, 32, 32), bf)
    xb[2].start()
    RB[at.s] = B[at.s]
    gs.rest()
    T[...] = K[...].T
    Qs[...] = (Q[...].astype(f32) * (Oa[:, 96:97] * SC)).astype(bf)

    mine = 8 + at.dp
    for part in range(3):
        xb[part].wait_recv()
        for j in range(4 * part, min(4 * part + 4, 9)):
            AG[mine, 32 * j:32 * j + 32, :] = jnp.concatenate(
                [RB[h, :, 96 * j:96 * j + 96] for h in range(16)], axis=1)
    gr = Gather(at, AG, 8, ss_h, rs_h)
    gr.own_out()
    gs.far()
    for kk in range(4):
        gs.other(kk)
    for w in weights:
        w.wait()

    def chunk(c, slot):
        for f in range(2):
            fs = slice(256 * f, 256 * f + 256)
            rows = AG[8 + c]
            gate = nn(rows, wg[:, fs])
            up = nn(rows, wu[:, fs])
            dact = nt(AG[c], wd[fs, :])
            sig = 1.0 / (1.0 + jnp.exp(-gate))
            silu = gate * sig
            ACT[c, :, fs] = (silu * up).astype(bf)
            DG[:, 256 * f:256 * f + 256] = (dact * up * (sig * (1.0 + gate * (1.0 - sig)))).astype(bf)
            DG[:, 512 + 256 * f:768 + 256 * f] = (dact * silu).astype(bf)
        for n in range(3):
            ns = slice(512 * n, 512 * n + 512)
            PT[slot, :, ns] = (nt(DG[:, :512], wg[ns, :]) + nt(DG[:, 512:], wu[ns, :])).astype(bf)

    def sib(k, slot):
        return rcopy(PT.at[slot], SR.at[k], ss_p.at[k], rs_p.at[k], (at.pair(0), at.s))

    order = (0, 1, 3, 2)

    def work(k):
        n = order.index(k)
        if n >= 2:
            sib(order[n - 2], n % 2).wait_send()
        chunk(at.pair(k), n % 2)
        sib(k, n % 2).start()
        chunk(at.clip(k), 2)
        sib(k, n % 2).wait_recv()
        SS[k] = (PT[2].astype(f32) + SR[k].astype(f32)).astype(bf)

    def half(k, i):
        return SS.at[k, pl.ds(144 * i, 144), :]

    msg = {"d1": (half(1, 1), 0, 1), "d3": (half(3, 0), 1, 3), "r1": (half(2, 0), 2, 1), "r3": (half(2, 1), 3, 3),
           "f1": (half(1, 0), 4, 1), "f3": (half(3, 1), 5, 3)}

    def hop(name):
        src, n, k = msg[name]
        return rcopy(src, RR.at[n], ss_r.at[n], rs_r.at[n], (at.clip(k), at.s))

    gr.other(0)
    work(0)
    gr.relay()
    gr.rest()
    gr.other(1)
    work(1)
    hop("d1").start()
    gr.far()
    gr.other(3)
    work(3)
    hop("d3").start()
    gr.other(2)
    work(2)
    hop("r1").start()
    hop("r3").start()
    acts = ACT[...].reshape(2304, 512)
    for n in range(3):
        ns = slice(512 * n, 512 * n + 512)
        grad_down[:, ns] = tn(acts, AG[0:8, :, ns].reshape(2304, 512)).astype(bf)
    hop("r1").wait_recv()
    SS[1, 0:144, :] = (SS[1, 0:144, :].astype(f32) + RR[2].astype(f32)).astype(bf)
    hop("f1").start()
    hop("r3").wait_recv()
    SS[3, 144:288, :] = (SS[3, 144:288, :].astype(f32) + RR[3].astype(f32)).astype(bf)
    hop("f3").start()
    for e in xb + xq:
        e.wait_send()
    gs.wait_send()
    gr.wait_send()
    hop("d3").wait_recv()
    hop("f1").wait_recv()
    SS[0, 0:144, :] = (SS[0, 0:144, :].astype(f32) + (RR[1].astype(f32) + RR[4].astype(f32))).astype(bf)
    hop("d1").wait_recv()
    hop("f3").wait_recv()
    SS[0, 144:288, :] = (SS[0, 144:288, :].astype(f32) + (RR[0].astype(f32) + RR[5].astype(f32))).astype(bf)

    xc = []
    for part in range(3):
        cols = pl.ds(384 * part, 384 if part < 2 else 128)
        xc.append(Exchange(at, lambda t, cols=cols: B.at[t, :, cols], lambda t, cols=cols: RB2.at[t, :, cols],
                           ss_c.at[part], rs_c.at[part]))
        for h in range(16):
            parts = [SS[0, 32 * j:32 * j + 32, 96 * h:96 * h + 96] for j in range(4 * part, min(4 * part + 4, 9))]
            if part == 2:
                parts.append(jnp.zeros((32, 32), bf))
            B[h, :, 384 * part:384 * part + (384 if part < 2 else 128)] = jnp.concatenate(parts, axis=1)
        xc[part].start()
    RB2[at.s] = B[at.s]
    xg.wait_recv()
    for part in range(2):
        xc[part].wait_recv()
        for j in range(4 * part, 4 * part + 4):
            for i in (0, 1):
                b = 2 * j + i
                w = RB2[:, 16 * i:16 * i + 16, 96 * j:96 * j + 96].reshape(256, 96)
                s_ref[128 * b:128 * b + 128, :96] = tn(main_places(M, b), w)
    xc[2].wait_recv()
    extra = RB2[:, :, 768:896].reshape(512, 128)
    for b in range(16):
        t = slice(128 * b, 128 * b + 128)
        gb = jnp.concatenate([RG[b, :, 96 * g:96 * g + 96] for g in range(4)], axis=0).astype(f32)
        dm = gb + (s_ref[t, :96] + tn(extra_places(M, b), extra)[:, :96])
        X[t, :] = jnp.concatenate([dm.astype(bf), jnp.zeros((128, 32), bf)], axis=1)

    dOs, dX = Q, K
    xo = [Exchange(at, lambda t, n=n: S.at[n, t], lambda t, n=n: R.at[n, t], ss_y.at[n], rs_y.at[n])
          for n in range(3)]

    def send_out(n):
        @pl.loop(0, 16)
        def _(b):
            S[n, b] = jnp.concatenate(
                [dX[pl.ds(pl.multiple_of(b * 128 + 32 * g, 32), 32), :96] for g in range(4)], axis=1)
        R[n, at.s] = S[n, at.s]
        xo[n].start()

    scale_back(X, Oa, dOs)

    @pl.loop(0, 4)
    def _(i):
        r = pl.ds(pl.multiple_of(i * 512, 512), 512)
        dX[r, :] = nn(ET[r, :], dOs[...]).astype(bf)
    send_out(2)
    for j in range(8):
        dscores(j, X, V, T, ET, Oa, AG, dX)
    send_out(0)
    for kb in range(8):
        slot, lane = dscore_at(6, kb)
        dX[256 * kb:256 * kb + 256, :] = (
            nn(AG[kb, 0:256, :], Qs[0:1536, :]) + nn(AG[slot, 0:256, lane:lane + 512], Qs[1536:2048, :])).astype(bf)
    send_out(1)
    for n in (2, 0, 1):
        xo[n].wait_recv()
    for e in [xm, xs, xe, xg] + xc + xo:
        e.wait_send()
    for k, n in ((3, 0), (2, 1)):
        sib(k, n).wait_send()
    for name in msg:
        hop(name).wait_send()


def results(R, gq, gk, gv):
    for n, dst in enumerate((gq, gk, gv)):
        for g in range(4):
            dst[32 * g:32 * g + 32, :] = jnp.concatenate(
                [R[n, h, :, 96 * g:96 * g + 96] for h in range(16)], axis=1)


def vm(*shape, dtype=bf):
    return pltpu.VMEM(shape, dtype)


def dma(*shape):
    return pltpu.SemaphoreType.DMA(shape)


def sds(*shape):
    return jax.ShapeDtypeStruct(shape, bf)


ANY = pl.BlockSpec(memory_space=pl.ANY)
VM = pl.BlockSpec(memory_space=pltpu.VMEM)


def per_device(query, key_in, value, grad_out, expert_ids, gate_weights, w_gate, w_up, w_down):
    head = [vm(2048, 128)] * 3 + [vm(128, 2048)] + [vm(2048, 128)] * 2
    R, gd = pl.pallas_call(
        block,
        out_shape=[sds(3, 16, 32, 384), sds(512, 1536)],
        in_specs=[VM] * 6 + [ANY] * 3,
        out_specs=[VM, VM],
        scratch_shapes=[
            vm(3, 16, 32, 384), vm(16, 32, 384), vm(16, 32, 384), vm(8, 128, dtype=f32), vm(16, 8, 128, dtype=f32),
            vm(16, 16, 1536), vm(16, 16, 1536), vm(16, 32, 128), vm(16, 32, 128),
            vm(16, 32, 896), vm(16, 32, 896), vm(16, 32, 896),
            vm(1536, 512), vm(1536, 512), vm(512, 1536), vm(16, 288, 1536), vm(2048, 2048)]
        + head + [vm(2048, 128, dtype=f32), vm(2048, 256, dtype=f32),
                  vm(8, 288, 512), vm(288, 1024), vm(3, 288, 1536), vm(4, 288, 1536), vm(4, 288, 1536),
                  vm(6, 144, 1536)]
        + [dma(4, 16)] * 2 + [dma(3, 16)] * 2 + [dma(16)] * 6 + [dma(3, 16)] * 4 + [dma(14)] * 4
        + [dma(4)] * 2 + [dma(6)] * 2 + [dma(3)],
        name="block",
        compiler_params=pltpu.CompilerParams(collective_id=0, has_side_effects=True, vmem_limit_bytes=VLIM),
    )(query[0], key_in[0], value[0], grad_out[0], expert_ids[0].T, gate_weights[0].T, w_gate[0], w_up[0], w_down[0])
    gq, gk, gv = pl.pallas_call(
        results,
        out_shape=[sds(128, 1536)] * 3,
        name="results",
    )(R)
    return (gq[None], gk[None], gv[None], gd[None])


def solution(mesh):
    seq = P("dp", "seq", None)
    return jax.shard_map(
        per_device,
        mesh=mesh,
        in_specs=(seq,) * 6 + (P("seq", None, "dp"), P("seq", None, "dp"), P("seq", "dp", None)),
        out_specs=(seq, seq, seq, P("seq", "dp", None)),
        check_vma=False,
    )
```

```python
import jax
import jax.numpy as jnp
from jax import lax
from jax.experimental import pallas as pl
from jax.experimental.pallas import tpu as pltpu
from jax.sharding import PartitionSpec as P

bf = jnp.bfloat16
f32 = jnp.float32
MESH = pl.DeviceIdType.MESH
HD = 96
SC = HD ** -0.5
C2 = SC * 1.4426950408889634
VLIM = 62 << 20
ORDER = [1, 4, 3, 12, 5, 15, 7, 13, 8, 2, 9, 6, 11, 14, 10]


def nt(a, b):
    return lax.dot_general(a, b, (((1,), (1,)), ((), ())), preferred_element_type=f32)


def nn(a, b):
    return lax.dot_general(a, b, (((1,), (0,)), ((), ())), preferred_element_type=f32)


def tn(a, b):
    return lax.dot_general(a, b, (((0,), (0,)), ((), ())), preferred_element_type=f32)


def iota(shape, dim):
    return lax.broadcasted_iota(jnp.int32, shape, dim)


def onehot(cond):
    return jnp.where(cond, 1.0, 0.0).astype(bf)


class Place:
    def __init__(self):
        self.dp = lax.axis_index("dp")
        self.s = lax.axis_index("seq")
        self.x = self.s // 4
        self.z = lax.rem(self.s, 4)
        self.y = self.dp // 2
        self.core = lax.rem(self.dp, 2)

    def to(self, o):
        dx, dz = o // 4, lax.rem(o, 4) if not isinstance(o, int) else o % 4
        return lax.rem(self.x + dx, 4) * 4 + lax.rem(self.z + dz, 4)

    def source(self, o):
        dx, dz = o // 4, lax.rem(o, 4) if not isinstance(o, int) else o % 4
        return lax.rem(self.x + 4 - dx, 4) * 4 + lax.rem(self.z + 4 - dz, 4)

    def clip(self, k):
        return lax.rem(self.y + k, 4) * 2 + self.core

    def pair(self, k):
        return lax.rem(self.y + k, 4) * 2 + 1 - self.core


def greet(devices):
    b = pltpu.get_barrier_semaphore()
    for d in devices:
        pl.semaphore_signal(b, inc=1, device_id=d, device_id_type=MESH)


def greeted(n):
    pl.semaphore_wait(pltpu.get_barrier_semaphore(), n)


def rcopy(src, dst, ss, rs, dev):
    return pltpu.make_async_remote_copy(
        src_ref=src, dst_ref=dst, send_sem=ss, recv_sem=rs, device_id=dev, device_id_type=MESH
    )


class Exchange:
    def __init__(self, at, send, recv, ss, rs):
        self.at, self.send, self.recv, self.ss, self.rs = at, send, recv, ss, rs

    def out(self, o):
        t = self.at.to(o)
        return rcopy(self.send(t), self.recv(self.at.s), self.ss.at[o], self.rs.at[o], (self.at.dp, t))

    def into(self, o):
        t = self.at.source(o)
        return rcopy(self.send(t), self.recv(t), self.ss.at[o], self.rs.at[o], (self.at.dp, t))

    def start(self):
        for o in ORDER:
            self.out(o).start()

    def wait_recv(self):
        @pl.loop(1, 16)
        def _(o):
            self.into(o).wait_recv()

    def wait_send(self):
        @pl.loop(1, 16)
        def _(o):
            self.out(o).wait_send()


def seq_peers(at):
    return [(at.dp, at.to(o)) for o in ORDER]


def dp_peers(at):
    return [(at.clip(1), at.s), (at.clip(3), at.s), (at.clip(2), at.s), (at.pair(0), at.s)]


def main_places(M, b):
    io = iota((256, 128), 0).astype(f32)
    return onehot((io == M[b, 0:1, :]) | (io == M[b, 1:2, :]))


def extra_places(M, b):
    io = iota((512, 128), 0)
    low = lax.rem(io, 32)
    own = (low // 2) == b
    tgt = ((io // 32) * 2 + lax.rem(io, 2)).astype(f32)
    return onehot(own & ((tgt == M[b, 2:3, :]) | (tgt == M[b, 3:4, :])))


class Gather:
    def __init__(self, at, buf, base, pieces, ss, rs):
        self.at, self.buf, self.base, self.pieces, self.ss, self.rs = at, buf, base, pieces, ss, rs

    def copy(self, n, c, i, dev):
        rows, cols = self.pieces[i]
        ref = self.buf.at[self.base + c, rows, cols]
        return rcopy(ref, ref, self.ss.at[n], self.rs.at[n], (dev, self.at.s))

    def own_out(self, i):
        a = self.at
        self.copy(i, a.clip(0), i, a.clip(1)).start()
        self.copy(2 + i, a.clip(0), i, a.clip(3)).start()
        self.copy(6 + i, a.clip(0), i, a.pair(0)).start()

    def near(self, i):
        a = self.at
        self.copy(i, a.clip(3), i, a.clip(1)).wait_recv()
        if i == 0:
            self.copy(4, a.clip(3), 0, a.clip(1)).start()
        self.copy(8 + i, a.clip(3), i, a.pair(0)).start()
        self.copy(2 + i, a.clip(1), i, a.clip(3)).wait_recv()
        if i == 1:
            self.copy(5, a.clip(1), 1, a.clip(3)).start()
        self.copy(10 + i, a.clip(1), i, a.pair(0)).start()

    def far(self):
        a = self.at
        for i in (0, 1):
            self.copy(4 + i, a.clip(2), i, a.clip(1)).wait_recv()
            self.copy(12 + i, a.clip(2), i, a.pair(0)).start()

    def other(self, k):
        n = {0: 6, 3: 8, 1: 10, 2: 12}[k]
        for i in (0, 1):
            self.copy(n + i, self.at.pair(k), i, self.at.pair(0)).wait_recv()

    def wait_send(self):
        for n in range(14):
            i = {4: 0, 5: 1}.get(n, n % 2)
            self.copy(n, self.at.clip(0), i, self.at.clip(1)).wait_send()


def scores(j, Q, K, ET, s_ref):
    CH = 512
    q0 = pl.multiple_of(j * 256, 256)
    Qj = Q[pl.ds(q0, 256), :]
    m = None
    for c in range(2048 // CH):
        s = nt(K[c * CH:(c + 1) * CH, :], Qj)
        s_ref[c * CH:(c + 1) * CH, :] = s
        mc = jnp.max(s.reshape(CH // 8, 8, 256), axis=0)
        m = mc if m is None else jnp.maximum(m, mc)
    m = jnp.max(m, axis=0, keepdims=True) * C2
    for c in range(2048 // CH):
        e = jnp.exp2(s_ref[c * CH:(c + 1) * CH, :] * C2 - m).astype(bf)
        ET[c * CH:(c + 1) * CH, pl.ds(q0, 256)] = e


def mix(j, Vt, ET, Oa, mixed):
    q0 = pl.multiple_of(j * 256, 256)
    ot = nn(Vt[...], ET[:, pl.ds(q0, 256)])
    linv = 1.0 / ot[96:97, :]
    on = jnp.concatenate([ot[:96, :] * linv, jnp.broadcast_to(linv, (32, 256))], axis=0)
    o = on.T
    Oa[pl.ds(q0, 256), :] = o
    mixed[pl.ds(q0, 256), :] = o.astype(bf)


def dscores(j, dO, V, Kt, ET, Oa, AG, dOs):
    r = pl.ds(pl.multiple_of(256 * j, 256), 256)
    d = dO[r, :96].astype(f32)
    oa = Oa[r, :]
    dOs[r, :] = jnp.concatenate([(d * oa[:, 96:97]).astype(bf), jnp.zeros((256, 32), bf)], axis=1)
    delta = -jnp.sum(d * oa[:, :96], axis=1, keepdims=True)
    hi = delta.astype(bf)
    rest = delta - hi.astype(f32)
    mid = rest.astype(bf)
    lo = (rest - mid.astype(f32)).astype(bf)
    daug = jnp.concatenate([d.astype(bf), hi, mid, lo, jnp.zeros((256, 29), bf)], axis=1)
    dqt = None
    for kb in range(8):
        ks = slice(256 * kb, 256 * kb + 256)
        ds = ET[ks, r] * nt(V[ks, :], daug).astype(bf)
        slot = jnp.where(j < 6, kb, 8 + kb // 3)
        lane = jnp.where(j < 6, 256 * j, 512 * (kb % 3) + 256 * (j - 6))
        AG[slot, 0:256, pl.ds(pl.multiple_of(lane, 256), 256)] = ds
        term = nn(Kt[:, ks], ds)
        dqt = term if dqt is None else dqt + term
    return (dqt.T * (oa[:, 96:97] * SC)).astype(bf)


def block(q, k, v, go, ids, gws, wg_hbm, wu_hbm, wd_hbm, R, grad_down,
          S, SG, RG, Ms, M, SM, RM, SX, RX, B, RB, RB2, wg, wu, wd, AG, ET, Q, K, V, T, X, Qs, Oa, s_ref,
          ACT, DG, PT, SR, SS, RR, gd,
          ss_x, rs_x, ss_y, rs_y, ss_m, rs_m, ss_s, rs_s, ss_e, rs_e, ss_b, rs_b, ss_c, rs_c, ss_g, rs_g, ss_h, rs_h,
          ss_p, rs_p, ss_r, rs_r, sem_w):
    at = Place()
    greet(seq_peers(at) + dp_peers(at))
    weights = [pltpu.make_async_copy(a, b, sem_w.at[n])
               for n, (a, b) in enumerate(((wg_hbm, wg), (wu_hbm, wu), (wd_hbm, wd)))]

    e0, e1 = ids[0:1, :].astype(f32), ids[1:2, :].astype(f32)
    g0, g1 = gws[0:1, :], gws[1:2, :]
    ie = iota((16, 128), 0).astype(f32)
    oh0, oh1 = jnp.where(ie == e0, 1.0, 0.0), jnp.where(ie == e1, 1.0, 0.0)
    before = onehot(iota((128, 128), 0) < iota((128, 128), 1))
    count = nn((oh0 + oh1).astype(bf), before)
    s0 = jnp.sum(oh0 * count, axis=0, keepdims=True)
    s1 = jnp.sum(oh1 * count, axis=0, keepdims=True)
    m0 = jnp.where(s0 < 16, e0 * 16 + s0, -1.0)
    m1 = jnp.where(s1 < 16, e1 * 16 + s1, -1.0)
    x0 = jnp.where(s0 < 16, -1.0, e0 * 2 + s0 - 16)
    x1 = jnp.where(s1 < 16, -1.0, e1 * 2 + s1 - 16)
    Ms[...] = jnp.concatenate([m0, m1, x0, x1, m0, m0, m0, m0], axis=0)

    io = iota((256, 128), 0).astype(f32)
    c0, c1 = io == m0, io == m1
    gw = jnp.sum(jnp.where(c0, g0, 0.0) + jnp.where(c1, g1, 0.0), axis=1, keepdims=True)
    pm = onehot(c0 | c1)
    for n in range(3):
        cols = slice(512 * n, 512 * n + 512)
        SM[:, :, cols] = (nn(pm, go[:, cols]) * gw).astype(bf).reshape(16, 16, 512)
    io = iota((32, 128), 0).astype(f32)
    c0, c1 = io == x0, io == x1
    gw = jnp.sum(jnp.where(c0, g0, 0.0) + jnp.where(c1, g1, 0.0), axis=1, keepdims=True)
    ext = (nn(onehot(c0 | c1), go[...]) * gw).astype(bf)
    stack = jnp.concatenate([ext[:, 128 * g:128 * g + 128] for g in range(12)], axis=0)
    r, c = iota((512, 384), 0), iota((512, 384), 1)
    low = lax.rem(r, 32)
    spread = onehot(c == (low // 2) * 32 + (r // 32) * 2 + lax.rem(low, 2))
    SX[...] = nn(spread, stack).astype(bf).reshape(16, 32, 128)

    xm = Exchange(at, lambda t: Ms, lambda t: M.at[t], ss_m, rs_m)
    halves = [pl.ds(0, 768), pl.ds(768, 768)]
    xs = [Exchange(at, lambda t, c=c: SM.at[t, :, c], lambda t, c=c: RM.at[t, :, c], ss_s.at[n], rs_s.at[n])
          for n, c in enumerate(halves)]
    xe = Exchange(at, lambda t: SX.at[t], lambda t: RX.at[t], ss_e, rs_e)
    xq = [Exchange(at, lambda t, n=n: S.at[n, t], lambda t, n=n: R.at[n, t], ss_x.at[n], rs_x.at[n])
          for n in range(3)]
    xg = Exchange(at, lambda t: SG.at[t], lambda t: RG.at[t], ss_x.at[3], rs_x.at[3])

    def pack(ref, put):
        for h in range(16):
            put(h, jnp.concatenate(
                [ref[32 * g:32 * g + 32, 96 * h:96 * h + 96] for g in range(4)], axis=1))

    greeted(19)
    xe.start()
    for e in xs:
        e.start()
    for n, ref in ((1, k), (0, q), (2, v)):
        def put(h, w):
            S[n, h] = w
        pack(ref, put)
        R[n, at.s] = S[n, at.s]
        if n < 2:
            xq[n].start()
    xm.start()

    def put_g(h, w):
        SG[h] = w
    pack(go, put_g)
    RG[at.s] = SG[at.s]
    for w in weights:
        w.start()
    M[at.s] = Ms[...]
    RM[at.s] = SM[at.s]
    RX[at.s] = SX[at.s]

    r, c = iota((384, 512), 1), iota((384, 512), 0)
    low = lax.rem(r, 32)
    pick = onehot(c == (low // 2) * 32 + (r // 32) * 2 + lax.rem(low, 2))
    xe.wait_recv()
    back = nn(pick, RX[...].reshape(512, 128)).astype(bf)
    AG[at.dp, 256:288, :] = jnp.concatenate([back[32 * g:32 * g + 32] for g in range(12)], axis=1)
    gs = Gather(at, AG, 0, [(pl.ds(0, 288), c) for c in halves], ss_g, rs_g)
    for i in (0, 1):
        xs[i].wait_recv()
        cols = slice(768 * i, 768 * i + 768)
        AG[at.dp, 0:256, cols] = RM[:, :, cols].reshape(256, 768)
        gs.own_out(i)

    def unpack(n, dst, fill):
        @pl.loop(0, 16)
        def _(b):
            w = R[n, b]
            for g in range(4):
                dst[pl.ds(pl.multiple_of(b * 128 + 32 * g, 32), 32), :] = jnp.concatenate(
                    [w[:, 96 * g:96 * g + 96], jnp.full((32, 32), fill, bf)], axis=1)

    xq[1].wait_recv()
    unpack(1, K, 0)
    xq[0].wait_recv()
    xq[2].start()
    unpack(0, Q, 0)

    @pl.loop(0, 8)
    def _(j):
        scores(j, Q, K, ET, s_ref)
    gs.near(0)
    xq[2].wait_recv()
    unpack(2, V, 1)
    T[...] = V[...].T
    xm.wait_recv()

    xb = []
    for part in range(3):
        cols = pl.ds(384 * part, 384 if part < 2 else 128)
        xb.append(Exchange(at, lambda t, cols=cols: B.at[t, :, cols], lambda t, cols=cols: RB.at[t, :, cols],
                           ss_b.at[part], rs_b.at[part]))
    for part in (0, 1):
        @pl.loop(4 * part, 4 * part + 4)
        def _(j):
            mix(j, T, ET, Oa, X)
        for j in range(4 * part, 4 * part + 4):
            for i in (0, 1):
                b = 2 * j + i
                w = nn(main_places(M, b), X[128 * b:128 * b + 128, :]).astype(bf)
                B[:, 16 * i:16 * i + 16, 96 * j:96 * j + 96] = w[:, :96].reshape(16, 16, 96)
        xb[part].start()
    acc = jnp.zeros((512, 128), f32)
    for b in range(16):
        acc = acc + nn(extra_places(M, b), X[128 * b:128 * b + 128, :])
    B[:, :, 768:864] = acc[:, :96].astype(bf).reshape(16, 32, 96)
    B[:, :, 864:896] = jnp.zeros((16, 32, 32), bf)
    xb[2].start()
    RB[at.s] = B[at.s]
    xg.start()
    gs.near(1)
    T[...] = K[...].T
    Qs[...] = (Q[...].astype(f32) * (Oa[:, 96:97] * SC)).astype(bf)

    mine = 8 + at.dp
    gr = Gather(at, AG, 8, [(pl.ds(0, 128), pl.ds(0, 1536)), (pl.ds(128, 160), pl.ds(0, 1536))], ss_h, rs_h)
    for part in range(3):
        xb[part].wait_recv()
        for j in range(4 * part, min(4 * part + 4, 9)):
            AG[mine, 32 * j:32 * j + 32, :] = jnp.concatenate(
                [RB[h, :, 96 * j:96 * j + 96] for h in range(16)], axis=1)
        if part == 0:
            gr.own_out(0)
    gr.own_out(1)
    gs.far()
    for kk in range(4):
        gs.other(kk)
    for w in weights:
        w.wait()

    def chunk(c, slot):
        for f in range(2):
            fs = slice(256 * f, 256 * f + 256)
            rows = AG[8 + c]
            gate = nn(rows, wg[:, fs])
            up = nn(rows, wu[:, fs])
            dact = nt(AG[c], wd[fs, :])
            sig = 1.0 / (1.0 + jnp.exp(-gate))
            silu = gate * sig
            ACT[c, :, fs] = (silu * up).astype(bf)
            DG[:, 256 * f:256 * f + 256] = (dact * up * (sig * (1.0 + gate * (1.0 - sig)))).astype(bf)
            DG[:, 512 + 256 * f:768 + 256 * f] = (dact * silu).astype(bf)
        for n in range(3):
            ns = slice(512 * n, 512 * n + 512)
            PT[slot, :, ns] = (nt(DG[:, :512], wg[ns, :]) + nt(DG[:, 512:], wu[ns, :])).astype(bf)

    def sib(k, slot):
        return rcopy(PT.at[slot], SR.at[k], ss_p.at[k], rs_p.at[k], (at.pair(0), at.s))

    order = (0, 1, 3, 2)

    def work(k):
        n = order.index(k)
        if n >= 2:
            sib(order[n - 2], n % 2).wait_send()
        chunk(at.pair(k), n % 2)
        sib(k, n % 2).start()
        chunk(at.clip(k), 2)
        sib(k, n % 2).wait_recv()
        SS[k] = (PT[2].astype(f32) + SR[k].astype(f32)).astype(bf)

    FIRST, SECOND = ((0, 64), (64, 80)), ((192, 96), (144, 48))
    msg = {}

    def add_messages(name, k, parts, to):
        for i, (lo, size) in enumerate(parts):
            msg[name + "ab"[i]] = (k, pl.ds(lo, size), to, len(msg), pl.ds(lo % 144, size))

    add_messages("d1", 1, SECOND, 1)
    add_messages("d3", 3, FIRST, 3)
    add_messages("r1", 2, FIRST, 1)
    add_messages("r3", 2, SECOND, 3)
    add_messages("f1", 1, FIRST, 1)
    add_messages("f3", 3, SECOND, 3)

    def hop(name):
        k, rows, to, n, land = msg[name]
        return rcopy(SS.at[k, rows, :], RR.at[n // 2, land, :], ss_r.at[n], rs_r.at[n], (at.clip(to), at.s))

    def start(name):
        for i in "ab":
            hop(name + i).start()

    def plus(k, rows, *names):
        term = SS[k, rows, :].astype(f32)
        for name in names:
            term = term + RR[msg[name][3] // 2, msg[name][4], :].astype(f32)
        SS[k, rows, :] = term.astype(bf)

    gr.other(0)
    work(0)
    gr.near(0)
    gr.near(1)
    gr.other(1)
    work(1)
    start("d1")
    gr.other(3)
    work(3)
    start("d3")
    gr.far()
    gr.other(2)
    work(2)
    start("r1")
    start("r3")
    acts = ACT[...].reshape(2304, 512)
    for n in range(3):
        ns = slice(512 * n, 512 * n + 512)
        gd[:, ns] = tn(acts, AG[0:8, :, ns].reshape(2304, 512)).astype(bf)
    gd_copy = pltpu.make_async_copy(gd, grad_down, sem_w.at[0])
    gd_copy.start()
    for i in "ab":
        for r, f in (("r1", "f1"), ("r3", "f3")):
            hop(r + i).wait_recv()
            plus(msg[f + i][0], msg[f + i][1], r + i)
            hop(f + i).start()
    for e in xb + xq:
        e.wait_send()
    gs.wait_send()
    gr.wait_send()

    GROUPS = {0: (0, 1, 6, 7), 2: (8,), 1: (2, 3, 4, 5)}
    xc = {}
    for part in (0, 2, 1):
        lanes = 384 if part < 2 else 128
        cols = pl.ds(384 * part, lanes)
        xc[part] = Exchange(at, lambda t, cols=cols: B.at[t, :, cols], lambda t, cols=cols: RB2.at[t, :, cols],
                            ss_c.at[part], rs_c.at[part])
        if part < 2:
            for direct, relayed in (("d3", "f1"), ("d1", "f3")):
                names = [direct + "ab"[part], relayed + "ab"[part]]
                for name in names:
                    hop(name).wait_recv()
                plus(0, msg[names[0]][1], *names)
        for h in range(16):
            parts = [SS[0, 32 * j:32 * j + 32, 96 * h:96 * h + 96] for j in GROUPS[part]]
            if part == 2:
                parts.append(jnp.zeros((32, 32), bf))
            B[h, :, 384 * part:384 * part + lanes] = jnp.concatenate(parts, axis=1)
        xc[part].start()
    RB2[at.s] = B[at.s]
    xg.wait_recv()

    def dmixed(part):
        extra = RB2[:, :, 768:896].reshape(512, 128)
        for n, j in enumerate(GROUPS[part]):
            for i in (0, 1):
                b = 2 * j + i
                lane = 384 * part + 96 * n
                t = slice(128 * b, 128 * b + 128)
                w = RB2[:, 16 * i:16 * i + 16, lane:lane + 96].reshape(256, 96)
                gb = jnp.concatenate([RG[b, :, 96 * g:96 * g + 96] for g in range(4)], axis=0).astype(f32)
                dm = gb + (tn(main_places(M, b), w) + tn(extra_places(M, b), extra)[:, :96])
                X[t, :] = jnp.concatenate([dm.astype(bf), jnp.zeros((128, 32), bf)], axis=1)

    dOs = Q
    def message(n, source, target):
        return rcopy(S.at[n, target], R.at[n, source], ss_y.at[n, target], rs_y.at[n, source], (at.dp, target))

    def lay(n, rows, b):
        S[n, b] = jnp.concatenate([rows[32 * g:32 * g + 32, :96] for g in range(4)], axis=1)

    def post(n, rows, first, count):
        for i in range(count):
            b = first + i
            lay(n, rows[128 * i:128 * i + 128, :], b)

            @pl.when(b != at.s)
            def _():
                message(n, at.s, b).start()

            @pl.when(b == at.s)
            def _():
                R[n, b] = S[n, b]

    def queries(first, step):
        @pl.loop(0, 4)
        def _(i):
            j = first + i + step * (i // 2)
            dq = dscores(j, X, V, T, ET, Oa, AG, dOs)
            for n in (0, 1):
                lay(0, dq[128 * n:128 * n + 128, :], 2 * j + n)

    for part in (0, 2):
        xc[part].wait_recv()
    dmixed(0)
    queries(0, 4)
    xc[1].wait_recv()
    dmixed(1)
    queries(2, 0)
    R[0, at.s] = S[0, at.s]
    for o in ORDER:
        message(0, at.s, at.to(o)).start()

    @pl.loop(0, 4)
    def _(i):
        j = lax.rem(i + at.s // 4, 4)
        rows = pl.ds(pl.multiple_of(j * 512, 512), 512)
        post(2, nn(ET[rows, :], dOs[...]).astype(bf), 4 * j, 4)

    @pl.loop(0, 8)
    def _(i):
        kb = lax.rem(i + at.s // 2, 8)
        lane = pl.ds(pl.multiple_of(512 * lax.rem(kb, 3), 512), 512)
        dk = nn(AG[kb, 0:256, :], Qs[0:1536, :]) + nn(AG[8 + kb // 3, 0:256, lane], Qs[1536:2048, :])
        post(1, dk.astype(bf), 2 * kb, 2)

    @pl.loop(1, 16)
    def _(o):
        t = at.source(o)
        for n in range(3):
            message(n, t, t).wait_recv()

    @pl.loop(1, 16)
    def _(o):
        t = at.to(o)
        for n in range(3):
            message(n, at.s, t).wait_send()

    for e in [xm, xe, xg] + xs + [xc[part] for part in range(3)]:
        e.wait_send()
    for k, n in ((3, 0), (2, 1)):
        sib(k, n).wait_send()
    for name in msg:
        hop(name).wait_send()
    gd_copy.wait()


def results(R, gd, gq, gk, gv, gd_out):
    for n, dst in enumerate((gq, gk, gv)):
        for g in range(4):
            dst[32 * g:32 * g + 32, :] = jnp.concatenate(
                [R[n, h, :, 96 * g:96 * g + 96] for h in range(16)], axis=1)
    gd_out[...] = gd[...]


def vm(*shape, dtype=bf):
    return pltpu.VMEM(shape, dtype)


def dma(*shape):
    return pltpu.SemaphoreType.DMA(shape)


def sds(*shape):
    return jax.ShapeDtypeStruct(shape, bf)


ANY = pl.BlockSpec(memory_space=pl.ANY)
VM = pl.BlockSpec(memory_space=pltpu.VMEM)


def per_device(query, key_in, value, grad_out, expert_ids, gate_weights, w_gate, w_up, w_down):
    head = [vm(2048, 128)] * 3 + [vm(128, 2048)] + [vm(2048, 128)] * 2
    R, gd = pl.pallas_call(
        block,
        out_shape=[sds(3, 16, 32, 384), sds(512, 1536)],
        in_specs=[VM] * 6 + [ANY] * 3,
        out_specs=[VM, ANY],
        scratch_shapes=[
            vm(3, 16, 32, 384), vm(16, 32, 384), vm(16, 32, 384), vm(8, 128, dtype=f32), vm(16, 8, 128, dtype=f32),
            vm(16, 16, 1536), vm(16, 16, 1536), vm(16, 32, 128), vm(16, 32, 128),
            vm(16, 32, 896), vm(16, 32, 896), vm(16, 32, 896),
            vm(1536, 512), vm(1536, 512), vm(512, 1536), vm(16, 288, 1536), vm(2048, 2048)]
        + head + [vm(2048, 128, dtype=f32), vm(2048, 256, dtype=f32),
                  vm(8, 288, 512), vm(288, 1024), vm(3, 288, 1536), vm(4, 288, 1536), vm(4, 288, 1536),
                  vm(6, 144, 1536), vm(512, 1536)]
        + [dma(4, 16)] * 2 + [dma(3, 16)] * 2 + [dma(16)] * 2 + [dma(2, 16)] * 2 + [dma(16)] * 2 + [dma(3, 16)] * 4 + [dma(14)] * 4
        + [dma(4)] * 2 + [dma(12)] * 2 + [dma(3)],
        name="block",
        compiler_params=pltpu.CompilerParams(collective_id=0, has_side_effects=True, vmem_limit_bytes=VLIM),
    )(query[0], key_in[0], value[0], grad_out[0], expert_ids[0].T, gate_weights[0].T, w_gate[0], w_up[0], w_down[0])
    gq, gk, gv, gd = pl.pallas_call(
        results,
        out_shape=[sds(128, 1536)] * 3 + [sds(512, 1536)],
        name="results",
    )(R, gd)
    return (gq[None], gk[None], gv[None], gd[None])


def solution(mesh):
    seq = P("dp", "seq", None)
    return jax.shard_map(
        per_device,
        mesh=mesh,
        in_specs=(seq,) * 6 + (P("seq", None, "dp"), P("seq", None, "dp"), P("seq", "dp", None)),
        out_specs=(seq, seq, seq, P("seq", "dp", None)),
        check_vma=False,
    )
```

```python
import jax
import jax.numpy as jnp
from jax import lax
from jax.experimental import pallas as pl
from jax.experimental.pallas import tpu as pltpu
from jax.sharding import PartitionSpec as P

bf = jnp.bfloat16
f32 = jnp.float32
MESH = pl.DeviceIdType.MESH
HD = 96
SC = HD ** -0.5
C2 = SC * 1.4426950408889634
VLIM = 62 << 20
ORDER = [1, 4, 3, 12, 5, 15, 7, 13, 8, 2, 9, 6, 11, 14, 10]


def nt(a, b):
    return lax.dot_general(a, b, (((1,), (1,)), ((), ())), preferred_element_type=f32)


def nn(a, b):
    return lax.dot_general(a, b, (((1,), (0,)), ((), ())), preferred_element_type=f32)


def tn(a, b):
    return lax.dot_general(a, b, (((0,), (0,)), ((), ())), preferred_element_type=f32)


def iota(shape, dim):
    return lax.broadcasted_iota(jnp.int32, shape, dim)


def onehot(cond):
    return jnp.where(cond, 1.0, 0.0).astype(bf)


class Place:
    def __init__(self):
        self.dp = lax.axis_index("dp")
        self.s = lax.axis_index("seq")
        self.x = self.s // 4
        self.z = lax.rem(self.s, 4)
        self.y = self.dp // 2
        self.core = lax.rem(self.dp, 2)

    def to(self, o):
        dx, dz = o // 4, lax.rem(o, 4) if not isinstance(o, int) else o % 4
        return lax.rem(self.x + dx, 4) * 4 + lax.rem(self.z + dz, 4)

    def source(self, o):
        dx, dz = o // 4, lax.rem(o, 4) if not isinstance(o, int) else o % 4
        return lax.rem(self.x + 4 - dx, 4) * 4 + lax.rem(self.z + 4 - dz, 4)

    def clip(self, k):
        return lax.rem(self.y + k, 4) * 2 + self.core

    def pair(self, k):
        return lax.rem(self.y + k, 4) * 2 + 1 - self.core


def greet(devices):
    b = pltpu.get_barrier_semaphore()
    for d in devices:
        pl.semaphore_signal(b, inc=1, device_id=d, device_id_type=MESH)


def greeted(n):
    pl.semaphore_wait(pltpu.get_barrier_semaphore(), n)


def rcopy(src, dst, ss, rs, dev):
    return pltpu.make_async_remote_copy(
        src_ref=src, dst_ref=dst, send_sem=ss, recv_sem=rs, device_id=dev, device_id_type=MESH
    )


class Exchange:
    def __init__(self, at, send, recv, ss, rs):
        self.at, self.send, self.recv, self.ss, self.rs = at, send, recv, ss, rs

    def out(self, o):
        t = self.at.to(o)
        return rcopy(self.send(t), self.recv(self.at.s), self.ss.at[o], self.rs.at[o], (self.at.dp, t))

    def into(self, o):
        t = self.at.source(o)
        return rcopy(self.send(t), self.recv(t), self.ss.at[o], self.rs.at[o], (self.at.dp, t))

    def start(self):
        for o in ORDER:
            self.out(o).start()

    def wait_recv(self):
        @pl.loop(1, 16)
        def _(o):
            self.into(o).wait_recv()

    def wait_send(self):
        @pl.loop(1, 16)
        def _(o):
            self.out(o).wait_send()


def seq_peers(at):
    return [(at.dp, at.to(o)) for o in ORDER]


def dp_peers(at):
    return [(at.clip(1), at.s), (at.clip(3), at.s), (at.clip(2), at.s), (at.pair(0), at.s)]


def main_places(M, b):
    io = iota((256, 128), 0).astype(f32)
    return onehot((io == M[b, 0:1, :]) | (io == M[b, 1:2, :]))


def extra_places(M, b):
    io = iota((512, 128), 0)
    low = lax.rem(io, 32)
    own = (low // 2) == b
    tgt = ((io // 32) * 2 + lax.rem(io, 2)).astype(f32)
    return onehot(own & ((tgt == M[b, 2:3, :]) | (tgt == M[b, 3:4, :])))


class Gather:
    def __init__(self, at, buf, base, pieces, ss, rs):
        self.at, self.buf, self.base, self.pieces, self.ss, self.rs = at, buf, base, pieces, ss, rs

    def copy(self, n, c, i, dev):
        rows, cols = self.pieces[i]
        ref = self.buf.at[self.base + c, rows, cols]
        return rcopy(ref, ref, self.ss.at[n], self.rs.at[n], (dev, self.at.s))

    def own_out(self, i):
        a = self.at
        self.copy(i, a.clip(0), i, a.clip(1)).start()
        self.copy(2 + i, a.clip(0), i, a.clip(3)).start()
        self.copy(6 + i, a.clip(0), i, a.pair(0)).start()

    def near(self, i):
        a = self.at
        self.copy(i, a.clip(3), i, a.clip(1)).wait_recv()
        if i == 0:
            self.copy(4, a.clip(3), 0, a.clip(1)).start()
        self.copy(8 + i, a.clip(3), i, a.pair(0)).start()
        self.copy(2 + i, a.clip(1), i, a.clip(3)).wait_recv()
        if i == 1:
            self.copy(5, a.clip(1), 1, a.clip(3)).start()
        self.copy(10 + i, a.clip(1), i, a.pair(0)).start()

    def far(self):
        a = self.at
        for i in (0, 1):
            self.copy(4 + i, a.clip(2), i, a.clip(1)).wait_recv()
            self.copy(12 + i, a.clip(2), i, a.pair(0)).start()

    def other(self, k):
        n = {0: 6, 3: 8, 1: 10, 2: 12}[k]
        for i in (0, 1):
            self.copy(n + i, self.at.pair(k), i, self.at.pair(0)).wait_recv()

    def wait_send(self):
        for n in range(14):
            i = {4: 0, 5: 1}.get(n, n % 2)
            self.copy(n, self.at.clip(0), i, self.at.clip(1)).wait_send()


def scores(j, Q, K, ET, s_ref):
    CH = 512
    q0 = pl.multiple_of(j * 256, 256)
    Qj = Q[pl.ds(q0, 256), :]
    m = None
    for c in range(2048 // CH):
        s = nt(K[c * CH:(c + 1) * CH, :], Qj)
        s_ref[c * CH:(c + 1) * CH, :] = s
        mc = jnp.max(s.reshape(CH // 8, 8, 256), axis=0)
        m = mc if m is None else jnp.maximum(m, mc)
    m = jnp.max(m, axis=0, keepdims=True) * C2
    for c in range(2048 // CH):
        e = jnp.exp2(s_ref[c * CH:(c + 1) * CH, :] * C2 - m).astype(bf)
        ET[c * CH:(c + 1) * CH, pl.ds(q0, 256)] = e


def mix(j, Vt, ET, Oa, mixed):
    q0 = pl.multiple_of(j * 256, 256)
    ot = nn(Vt[...], ET[:, pl.ds(q0, 256)])
    linv = 1.0 / ot[96:97, :]
    on = jnp.concatenate([ot[:96, :] * linv, jnp.broadcast_to(linv, (32, 256))], axis=0)
    o = on.T
    Oa[pl.ds(q0, 256), :] = o
    mixed[pl.ds(q0, 256), :] = o.astype(bf)


def dscores(j, dO, V, ET, Oa, AG, dOs):
    r = pl.ds(pl.multiple_of(256 * j, 256), 256)
    d = dO[r, :96].astype(f32)
    oa = Oa[r, :]
    dOs[r, :] = jnp.concatenate([(d * oa[:, 96:97]).astype(bf), jnp.zeros((256, 32), bf)], axis=1)
    delta = -jnp.sum(d * oa[:, :96], axis=1, keepdims=True)
    hi = delta.astype(bf)
    rest = delta - hi.astype(f32)
    mid = rest.astype(bf)
    lo = (rest - mid.astype(f32)).astype(bf)
    daug = jnp.concatenate([d.astype(bf), hi, mid, lo, jnp.zeros((256, 29), bf)], axis=1)
    for kb in range(8):
        ks = slice(256 * kb, 256 * kb + 256)
        ds = ET[ks, r] * nt(V[ks, :], daug).astype(bf)
        slot = jnp.where(j < 6, kb, 8 + kb // 3)
        lane = jnp.where(j < 6, 256 * j, 512 * (kb % 3) + 256 * (j - 6))
        AG[slot, 0:256, pl.ds(pl.multiple_of(lane, 256), 256)] = ds


def dqueries(j, Kt, Oa, AG):
    r = pl.ds(pl.multiple_of(256 * j, 256), 256)
    dqt = None
    for kb in range(8):
        slot = jnp.where(j < 6, kb, 8 + kb // 3)
        lane = jnp.where(j < 6, 256 * j, 512 * (kb % 3) + 256 * (j - 6))
        term = nn(Kt[:, 256 * kb:256 * kb + 256], AG[slot, 0:256, pl.ds(pl.multiple_of(lane, 256), 256)])
        dqt = term if dqt is None else dqt + term
    return (dqt.T * (Oa[r, 96:97] * SC)).astype(bf)


def block(q, k, v, go, ids, gws, wg_hbm, wu_hbm, wd_hbm, R, grad_down,
          S, SG, RG, Ms, M, SM, RM, SX, RX, B, RB, RB2, wg, wu, wd, AG, ET, Q, K, V, T, X, Qs, Oa, s_ref,
          ACT, DG, PT, SR, SS, RR, gd,
          ss_x, rs_x, ss_y, rs_y, ss_m, rs_m, ss_s, rs_s, ss_e, rs_e, ss_b, rs_b, ss_c, rs_c, ss_g, rs_g, ss_h, rs_h,
          ss_p, rs_p, ss_r, rs_r, sem_w):
    at = Place()
    greet(seq_peers(at) + dp_peers(at))
    weights = [pltpu.make_async_copy(a, b, sem_w.at[n])
               for n, (a, b) in enumerate(((wg_hbm, wg), (wu_hbm, wu), (wd_hbm, wd)))]

    e0, e1 = ids[0:1, :].astype(f32), ids[1:2, :].astype(f32)
    g0, g1 = gws[0:1, :], gws[1:2, :]
    ie = iota((16, 128), 0).astype(f32)
    oh0, oh1 = jnp.where(ie == e0, 1.0, 0.0), jnp.where(ie == e1, 1.0, 0.0)
    before = onehot(iota((128, 128), 0) < iota((128, 128), 1))
    count = nn((oh0 + oh1).astype(bf), before)
    s0 = jnp.sum(oh0 * count, axis=0, keepdims=True)
    s1 = jnp.sum(oh1 * count, axis=0, keepdims=True)
    m0 = jnp.where(s0 < 16, e0 * 16 + s0, -1.0)
    m1 = jnp.where(s1 < 16, e1 * 16 + s1, -1.0)
    x0 = jnp.where(s0 < 16, -1.0, e0 * 2 + s0 - 16)
    x1 = jnp.where(s1 < 16, -1.0, e1 * 2 + s1 - 16)
    Ms[...] = jnp.concatenate([m0, m1, x0, x1, m0, m0, m0, m0], axis=0)

    io = iota((256, 128), 0).astype(f32)
    c0, c1 = io == m0, io == m1
    gw = jnp.sum(jnp.where(c0, g0, 0.0) + jnp.where(c1, g1, 0.0), axis=1, keepdims=True)
    pm = onehot(c0 | c1)
    for n in range(3):
        cols = slice(512 * n, 512 * n + 512)
        SM[:, :, cols] = (nn(pm, go[:, cols]) * gw).astype(bf).reshape(16, 16, 512)
    io = iota((32, 128), 0).astype(f32)
    c0, c1 = io == x0, io == x1
    gw = jnp.sum(jnp.where(c0, g0, 0.0) + jnp.where(c1, g1, 0.0), axis=1, keepdims=True)
    ext = (nn(onehot(c0 | c1), go[...]) * gw).astype(bf)
    stack = jnp.concatenate([ext[:, 128 * g:128 * g + 128] for g in range(12)], axis=0)
    r, c = iota((512, 384), 0), iota((512, 384), 1)
    low = lax.rem(r, 32)
    spread = onehot(c == (low // 2) * 32 + (r // 32) * 2 + lax.rem(low, 2))
    SX[...] = nn(spread, stack).astype(bf).reshape(16, 32, 128)

    xm = Exchange(at, lambda t: Ms, lambda t: M.at[t], ss_m, rs_m)
    halves = [pl.ds(0, 768), pl.ds(768, 768)]
    xs = [Exchange(at, lambda t, c=c: SM.at[t, :, c], lambda t, c=c: RM.at[t, :, c], ss_s.at[n], rs_s.at[n])
          for n, c in enumerate(halves)]
    xe = Exchange(at, lambda t: SX.at[t], lambda t: RX.at[t], ss_e, rs_e)
    xq = [Exchange(at, lambda t, n=n: S.at[n, t], lambda t, n=n: R.at[n, t], ss_x.at[n], rs_x.at[n])
          for n in range(3)]
    xg = Exchange(at, lambda t: SG.at[t], lambda t: RG.at[t], ss_x.at[3], rs_x.at[3])

    def pack(ref, put):
        for h in range(16):
            put(h, jnp.concatenate(
                [ref[32 * g:32 * g + 32, 96 * h:96 * h + 96] for g in range(4)], axis=1))

    greeted(19)
    xe.start()
    for e in xs:
        e.start()
    for n, ref in ((1, k), (0, q), (2, v)):
        def put(h, w):
            S[n, h] = w
        pack(ref, put)
        R[n, at.s] = S[n, at.s]
        if n < 2:
            xq[n].start()
    xm.start()

    def put_g(h, w):
        SG[h] = w
    pack(go, put_g)
    RG[at.s] = SG[at.s]
    for w in weights:
        w.start()
    M[at.s] = Ms[...]
    RM[at.s] = SM[at.s]
    RX[at.s] = SX[at.s]

    r, c = iota((384, 512), 1), iota((384, 512), 0)
    low = lax.rem(r, 32)
    pick = onehot(c == (low // 2) * 32 + (r // 32) * 2 + lax.rem(low, 2))
    xe.wait_recv()
    back = nn(pick, RX[...].reshape(512, 128)).astype(bf)
    AG[at.dp, 256:288, :] = jnp.concatenate([back[32 * g:32 * g + 32] for g in range(12)], axis=1)
    gs = Gather(at, AG, 0, [(pl.ds(0, 288), c) for c in halves], ss_g, rs_g)
    for i in (0, 1):
        xs[i].wait_recv()
        cols = slice(768 * i, 768 * i + 768)
        AG[at.dp, 0:256, cols] = RM[:, :, cols].reshape(256, 768)
        gs.own_out(i)

    def unpack(n, dst, fill):
        @pl.loop(0, 16)
        def _(b):
            w = R[n, b]
            for g in range(4):
                dst[pl.ds(pl.multiple_of(b * 128 + 32 * g, 32), 32), :] = jnp.concatenate(
                    [w[:, 96 * g:96 * g + 96], jnp.full((32, 32), fill, bf)], axis=1)

    xq[1].wait_recv()
    unpack(1, K, 0)
    xq[0].wait_recv()
    xq[2].start()
    unpack(0, Q, 0)

    @pl.loop(0, 8)
    def _(j):
        scores(j, Q, K, ET, s_ref)
    gs.near(0)
    xq[2].wait_recv()
    unpack(2, V, 1)
    T[...] = V[...].T
    xm.wait_recv()

    xb = []
    for part in range(3):
        cols = pl.ds(384 * part, 384 if part < 2 else 128)
        xb.append(Exchange(at, lambda t, cols=cols: B.at[t, :, cols], lambda t, cols=cols: RB.at[t, :, cols],
                           ss_b.at[part], rs_b.at[part]))
    for part in (0, 1):
        @pl.loop(4 * part, 4 * part + 4)
        def _(j):
            mix(j, T, ET, Oa, X)
        for j in range(4 * part, 4 * part + 4):
            for i in (0, 1):
                b = 2 * j + i
                w = nn(main_places(M, b), X[128 * b:128 * b + 128, :]).astype(bf)
                B[:, 16 * i:16 * i + 16, 96 * j:96 * j + 96] = w[:, :96].reshape(16, 16, 96)
        xb[part].start()
        if part == 0:
            gs.near(1)
    acc = jnp.zeros((512, 128), f32)
    for b in range(16):
        acc = acc + nn(extra_places(M, b), X[128 * b:128 * b + 128, :])
    B[:, :, 768:864] = acc[:, :96].astype(bf).reshape(16, 32, 96)
    B[:, :, 864:896] = jnp.zeros((16, 32, 32), bf)
    xb[2].start()
    RB[at.s] = B[at.s]
    xg.start()
    T[...] = K[...].T
    Qs[...] = (Q[...].astype(f32) * (Oa[:, 96:97] * SC)).astype(bf)

    mine = 8 + at.dp
    gr = Gather(at, AG, 8, [(pl.ds(0, 128), pl.ds(0, 1536)), (pl.ds(128, 160), pl.ds(0, 1536))], ss_h, rs_h)
    for part in range(3):
        xb[part].wait_recv()
        for j in range(4 * part, min(4 * part + 4, 9)):
            AG[mine, 32 * j:32 * j + 32, :] = jnp.concatenate(
                [RB[h, :, 96 * j:96 * j + 96] for h in range(16)], axis=1)
        if part == 0:
            gr.own_out(0)
    gr.own_out(1)
    gs.far()
    for kk in range(4):
        gs.other(kk)
    for w in weights:
        w.wait()

    def chunk(c, slot):
        for f in range(2):
            fs = slice(256 * f, 256 * f + 256)
            rows = AG[8 + c]
            gate = nn(rows, wg[:, fs])
            up = nn(rows, wu[:, fs])
            dact = nt(AG[c], wd[fs, :])
            sig = 1.0 / (1.0 + jnp.exp(-gate))
            silu = gate * sig
            ACT[c, :, fs] = (silu * up).astype(bf)
            DG[:, 256 * f:256 * f + 256] = (dact * up * (sig * (1.0 + gate * (1.0 - sig)))).astype(bf)
            DG[:, 512 + 256 * f:768 + 256 * f] = (dact * silu).astype(bf)
        for n in range(3):
            ns = slice(512 * n, 512 * n + 512)
            PT[slot, :, ns] = (nt(DG[:, :512], wg[ns, :]) + nt(DG[:, 512:], wu[ns, :])).astype(bf)

    def sib(k, slot):
        return rcopy(PT.at[slot], SR.at[k], ss_p.at[k], rs_p.at[k], (at.pair(0), at.s))

    order = (0, 1, 3, 2)

    def work(k):
        n = order.index(k)
        if n >= 2:
            sib(order[n - 2], n % 2).wait_send()
        chunk(at.pair(k), n % 2)
        sib(k, n % 2).start()
        chunk(at.clip(k), 2)
        sib(k, n % 2).wait_recv()
        SS[k] = (PT[2].astype(f32) + SR[k].astype(f32)).astype(bf)

    FIRST, SECOND = ((0, 64), (64, 80)), ((192, 96), (144, 48))
    msg = {}

    def add_messages(name, k, parts, to):
        for i, (lo, size) in enumerate(parts):
            msg[name + "ab"[i]] = (k, pl.ds(lo, size), to, len(msg), pl.ds(lo % 144, size))

    add_messages("d1", 1, SECOND, 1)
    add_messages("d3", 3, FIRST, 3)
    add_messages("r1", 2, FIRST, 1)
    add_messages("r3", 2, SECOND, 3)
    add_messages("f1", 1, FIRST, 1)
    add_messages("f3", 3, SECOND, 3)

    def hop(name):
        k, rows, to, n, land = msg[name]
        return rcopy(SS.at[k, rows, :], RR.at[n // 2, land, :], ss_r.at[n], rs_r.at[n], (at.clip(to), at.s))

    def start(name):
        for i in "ab":
            hop(name + i).start()

    def plus(k, rows, *names):
        term = SS[k, rows, :].astype(f32)
        for name in names:
            term = term + RR[msg[name][3] // 2, msg[name][4], :].astype(f32)
        SS[k, rows, :] = term.astype(bf)

    gr.other(0)
    work(0)
    gr.near(0)
    gr.near(1)
    gr.other(1)
    work(1)
    start("d1")
    gr.other(3)
    work(3)
    start("d3")
    gr.far()
    gr.other(2)
    work(2)
    start("r1")
    start("r3")
    acts = ACT[...].reshape(2304, 512)
    for n in range(3):
        ns = slice(512 * n, 512 * n + 512)
        gd[:, ns] = tn(acts, AG[0:8, :, ns].reshape(2304, 512)).astype(bf)
    gd_copy = pltpu.make_async_copy(gd, grad_down, sem_w.at[0])
    gd_copy.start()
    for i in "ab":
        for r, f in (("r1", "f1"), ("r3", "f3")):
            hop(r + i).wait_recv()
            plus(msg[f + i][0], msg[f + i][1], r + i)
            hop(f + i).start()
    for e in xb + xq:
        e.wait_send()
    gs.wait_send()
    gr.wait_send()

    GROUPS = {0: (0, 1, 6, 7), 2: (8,), 1: (2, 3, 4, 5)}
    xc = {}
    for part in (0, 2, 1):
        lanes = 384 if part < 2 else 128
        cols = pl.ds(384 * part, lanes)
        xc[part] = Exchange(at, lambda t, cols=cols: B.at[t, :, cols], lambda t, cols=cols: RB2.at[t, :, cols],
                            ss_c.at[part], rs_c.at[part])
        if part < 2:
            for direct, relayed in (("d3", "f1"), ("d1", "f3")):
                names = [direct + "ab"[part], relayed + "ab"[part]]
                for name in names:
                    hop(name).wait_recv()
                plus(0, msg[names[0]][1], *names)
        for h in range(16):
            parts = [SS[0, 32 * j:32 * j + 32, 96 * h:96 * h + 96] for j in GROUPS[part]]
            if part == 2:
                parts.append(jnp.zeros((32, 32), bf))
            B[h, :, 384 * part:384 * part + lanes] = jnp.concatenate(parts, axis=1)
        xc[part].start()
    RB2[at.s] = B[at.s]
    xg.wait_recv()

    def dmixed(part):
        extra = RB2[:, :, 768:896].reshape(512, 128)
        for n, j in enumerate(GROUPS[part]):
            for i in (0, 1):
                b = 2 * j + i
                lane = 384 * part + 96 * n
                t = slice(128 * b, 128 * b + 128)
                w = RB2[:, 16 * i:16 * i + 16, lane:lane + 96].reshape(256, 96)
                gb = jnp.concatenate([RG[b, :, 96 * g:96 * g + 96] for g in range(4)], axis=0).astype(f32)
                dm = gb + (tn(main_places(M, b), w) + tn(extra_places(M, b), extra)[:, :96])
                X[t, :] = jnp.concatenate([dm.astype(bf), jnp.zeros((128, 32), bf)], axis=1)

    dOs = Q
    def message(n, source, target):
        return rcopy(S.at[n, target], R.at[n, source], ss_y.at[n, target], rs_y.at[n, source], (at.dp, target))

    def lay(n, rows, b):
        S[n, b] = jnp.concatenate([rows[32 * g:32 * g + 32, :96] for g in range(4)], axis=1)

    def go_out(n, b):
        @pl.when(b != at.s)
        def _():
            message(n, at.s, b).start()

        @pl.when(b == at.s)
        def _():
            R[n, b] = S[n, b]

    def post(n, rows, first, count):
        for i in range(count):
            lay(n, rows[128 * i:128 * i + 128, :], first + i)
            go_out(n, first + i)

    for part in (0, 2):
        xc[part].wait_recv()
    dmixed(0)

    @pl.loop(0, 4)
    def _(i):
        dscores(i + 4 * (i // 2), X, V, ET, Oa, AG, dOs)

    @pl.loop(0, 4)
    def _(i):
        j = i + 4 * (i // 2)
        dq = dqueries(j, T, Oa, AG)
        for n in (0, 1):
            lay(0, dq[128 * n:128 * n + 128, :], 2 * j + n)

    xc[1].wait_recv()

    @pl.loop(0, 8)
    def _(i):
        n = lax.rem(i + at.s, 8)
        go_out(0, n + 8 * (n // 4))

    dmixed(1)

    @pl.loop(0, 4)
    def _(i):
        dscores(2 + i, X, V, ET, Oa, AG, dOs)

    @pl.loop(0, 4)
    def _(i):
        j = 2 + lax.rem(i + at.s, 4)
        post(0, dqueries(j, T, Oa, AG), 2 * j, 2)

    @pl.loop(0, 4)
    def _(i):
        j = lax.rem(i + at.s // 4, 4)
        rows = pl.ds(pl.multiple_of(j * 512, 512), 512)
        post(2, nn(ET[rows, :], dOs[...]).astype(bf), 4 * j, 4)

    @pl.loop(0, 8)
    def _(i):
        kb = lax.rem(i + at.s // 2, 8)
        lane = pl.ds(pl.multiple_of(512 * lax.rem(kb, 3), 512), 512)
        dk = nn(AG[kb, 0:256, :], Qs[0:1536, :]) + nn(AG[8 + kb // 3, 0:256, lane], Qs[1536:2048, :])
        post(1, dk.astype(bf), 2 * kb, 2)

    @pl.loop(1, 16)
    def _(o):
        t = at.source(o)
        for n in range(3):
            message(n, t, t).wait_recv()

    @pl.loop(1, 16)
    def _(o):
        t = at.to(o)
        for n in range(3):
            message(n, at.s, t).wait_send()

    for e in [xm, xe, xg] + xs + [xc[part] for part in range(3)]:
        e.wait_send()
    for k, n in ((3, 0), (2, 1)):
        sib(k, n).wait_send()
    for name in msg:
        hop(name).wait_send()
    gd_copy.wait()


def results(R, gd, gq, gk, gv, gd_out):
    for n, dst in enumerate((gq, gk, gv)):
        for g in range(4):
            dst[32 * g:32 * g + 32, :] = jnp.concatenate(
                [R[n, h, :, 96 * g:96 * g + 96] for h in range(16)], axis=1)
    gd_out[...] = gd[...]


def vm(*shape, dtype=bf):
    return pltpu.VMEM(shape, dtype)


def dma(*shape):
    return pltpu.SemaphoreType.DMA(shape)


def sds(*shape):
    return jax.ShapeDtypeStruct(shape, bf)


ANY = pl.BlockSpec(memory_space=pl.ANY)
VM = pl.BlockSpec(memory_space=pltpu.VMEM)


def per_device(query, key_in, value, grad_out, expert_ids, gate_weights, w_gate, w_up, w_down):
    head = [vm(2048, 128)] * 3 + [vm(128, 2048)] + [vm(2048, 128)] * 2
    R, gd = pl.pallas_call(
        block,
        out_shape=[sds(3, 16, 32, 384), sds(512, 1536)],
        in_specs=[VM] * 6 + [ANY] * 3,
        out_specs=[VM, ANY],
        scratch_shapes=[
            vm(3, 16, 32, 384), vm(16, 32, 384), vm(16, 32, 384), vm(8, 128, dtype=f32), vm(16, 8, 128, dtype=f32),
            vm(16, 16, 1536), vm(16, 16, 1536), vm(16, 32, 128), vm(16, 32, 128),
            vm(16, 32, 896), vm(16, 32, 896), vm(16, 32, 896),
            vm(1536, 512), vm(1536, 512), vm(512, 1536), vm(16, 288, 1536), vm(2048, 2048)]
        + head + [vm(2048, 128, dtype=f32), vm(2048, 256, dtype=f32),
                  vm(8, 288, 512), vm(288, 1024), vm(3, 288, 1536), vm(4, 288, 1536), vm(4, 288, 1536),
                  vm(6, 144, 1536), vm(512, 1536)]
        + [dma(4, 16)] * 2 + [dma(3, 16)] * 2 + [dma(16)] * 2 + [dma(2, 16)] * 2 + [dma(16)] * 2 + [dma(3, 16)] * 4 + [dma(14)] * 4
        + [dma(4)] * 2 + [dma(12)] * 2 + [dma(3)],
        name="block",
        compiler_params=pltpu.CompilerParams(collective_id=0, has_side_effects=True, vmem_limit_bytes=VLIM),
    )(query[0], key_in[0], value[0], grad_out[0], expert_ids[0].T, gate_weights[0].T, w_gate[0], w_up[0], w_down[0])
    gq, gk, gv, gd = pl.pallas_call(
        results,
        out_shape=[sds(128, 1536)] * 3 + [sds(512, 1536)],
        name="results",
    )(R, gd)
    return (gq[None], gk[None], gv[None], gd[None])


def solution(mesh):
    seq = P("dp", "seq", None)
    return jax.shard_map(
        per_device,
        mesh=mesh,
        in_specs=(seq,) * 6 + (P("seq", None, "dp"), P("seq", None, "dp"), P("seq", "dp", None)),
        out_specs=(seq, seq, seq, P("seq", "dp", None)),
        check_vma=False,
    )
```
